128 devices in a mesh: cfg: 2 (over z_lo), seq: 8 (over x, core), head: 8 (over y, z_hi).
Axes of the slice: x: 4, y: 4, z: 4 (z_hi: 2, z_lo: 2; z = z_hi * 2 + z_lo), core: 2. Of those that a mesh axis runs over, the one named last changes fastest.
Arguments:
- q_img: bfloat16 [2, 8192, 2560], P('cfg', ('seq', 'head')), may hold values from -240 to 240
- k_img: bfloat16 [2, 8192, 2560], P('cfg', ('seq', 'head')), may hold values from -6 to 6
- v_img: bfloat16 [2, 8192, 2560], P('cfg', ('seq', 'head')), may hold values from -6 to 6
- text_k: bfloat16 [2, 384, 2560], P('cfg'), may hold values from -6 to 6
- text_v: bfloat16 [2, 384, 2560], P('cfg'), may hold values from -6 to 6
- text_len: int32 [2], P('cfg'), may hold values from 1 to 384, as said below
- head_mask: int32 [40], replicated, may hold values 0 or 1
- hidden: bfloat16 [2, 8192, 2432], P('cfg', ('seq', 'head')), may hold values from -6 to 6
- out_weight: bfloat16 [2560, 2432], P('head'), may hold values from -0.125 to 0.125
- out_bias: bfloat16 [2432], replicated, may hold values from -3 to 3
- final_shift: bfloat16 [2, 2432], P('cfg'), may hold values from -3 to 3
- final_scale: bfloat16 [2, 2432], P('cfg'), may hold values from -1.5 to 1.5
- final_weight: bfloat16 [64, 2432], replicated, may hold values from -0.125 to 0.125
- latent: float32 [64, 8192], P('cfg', ('seq', 'head')), may hold values from -6 to 6
- step_index: int32 [1], replicated, may hold values from 0 to 27
Outputs:
- next_latent: float32 [64, 8192], P('cfg', ('seq', 'head'))
- denoised: float32 [64, 8192], P('cfg', ('seq', 'head'))
The draws below stay inside these ranges and needn't reach their ends.
Inputs may be any that keep to these rules, and one draw needn't show every extreme that they name: `text_len`: some branch has all 384 text tokens live.
All inputs are finite; a program needn't handle non-finite values.
Results may differ from the reference program's by a relative error of at most 0.0085.
Values may be sent and summed in bfloat16 or wider, within the bound.
A program may use at most 128 MiB of HBM per device.

```python
import math
import jax
import jax.numpy as jnp
from jax import lax

D = 2432
HEADS = 40
HDIM = 64
CH = 64
TXT = 384
STEPS = 28
HD = 2560
IMG = 8192


def image_keys(key):
    return jnp.clip(jax.random.normal(jax.random.fold_in(key, 11), (2, IMG, HD), jnp.float32), -6.0, 6.0)


def text_keys(key):
    return jnp.clip(jax.random.normal(jax.random.fold_in(key, 13), (2, TXT, HD), jnp.float32), -6.0, 6.0)


def draw_k_img(key, part):
    drawn = image_keys(key)
    return drawn.astype(jnp.bfloat16)


def draw_text_k(key, part):
    drawn = text_keys(key)
    return drawn.astype(jnp.bfloat16)


def draw_q_img(key, part):
    keys_drawn = image_keys(key)
    text_drawn = text_keys(key)
    key = jax.random.fold_in(key, 5)
    image_pick = jax.random.randint(jax.random.fold_in(key, 1), (2, IMG), 0, IMG)
    text_pick = jax.random.randint(jax.random.fold_in(key, 2), (2, IMG), 0, TXT)
    noise = 0.5 * jnp.clip(jax.random.normal(jax.random.fold_in(key, 3), (2, IMG, HD), jnp.float32), -6.0, 6.0)
    image_match = jnp.stack([keys_drawn[0][image_pick[0]], keys_drawn[1][image_pick[1]]])
    text_match = jnp.stack([text_drawn[0][text_pick[0]], text_drawn[1][text_pick[1]]])
    drawn = 1.25 * (image_match + text_match) + noise
    return drawn.astype(jnp.bfloat16)


def draw_text_len(key, part):
    key = jax.random.fold_in(key, 7)
    shorter = jax.random.randint(jax.random.fold_in(key, 1), (2,), 1, TXT + 1)
    full_branch = jax.random.randint(jax.random.fold_in(key, 2), (), 0, 2)
    return jnp.where(jnp.arange(2) == full_branch, TXT, shorter).astype(jnp.int32)


def with_ends(values, key, smallest, largest):
    shape = values.shape
    spot = [jax.random.randint(jax.random.fold_in(key, axis), (), 0, shape[axis]) for axis in range(len(shape))]
    values = values.at[tuple(spot)].set(smallest)
    longest = shape.index(max(shape))
    spot[longest] = (spot[longest] + 1) % shape[longest]
    return values.at[tuple(spot)].set(largest)


def shard_levels(own_key, dims, shards, smallest, high):
    loudness, own = 1.0, jax.random.fold_in(own_key, 6)
    for dim, blocks in shards:
        heights = jnp.exp(jax.random.uniform(jax.random.fold_in(own, dim), (blocks,), jnp.float32, smallest / len(shards), high / len(shards)))
        loudness = loudness * jnp.repeat(heights, dims[dim] // blocks).reshape([-1 if axis == dim else 1 for axis in range(len(dims))])
    return loudness


def normal_values(rng, shape, scale, most, split=(), held_as=jnp.bfloat16):
    array = jax.random.normal(rng, shape, jnp.float32) * scale
    if len(split) > 0:
        array = shard_levels(rng, shape, split, -0.22, 0.18) * array
    return jnp.clip(array, min=-most, max=most).astype(held_as)


def setup_inputs(seed: int = 0) -> dict:
    arg_keys = jax.random.split(jax.random.key(seed), 16)
    return {
        "q_img": draw_q_img(jax.random.fold_in(arg_keys[15], 71), 0),
        "k_img": draw_k_img(jax.random.fold_in(arg_keys[15], 71), 0),
        "v_img": normal_values(arg_keys[2], (2, IMG, HD), 1.0, 6.0, ((0, 2), (1, 64))),
        "text_k": draw_text_k(jax.random.fold_in(arg_keys[15], 71), 0),
        "text_v": normal_values(arg_keys[4], (2, TXT, HD), 1.0, 6.0, ((0, 2),)),
        "text_len": draw_text_len(jax.random.fold_in(arg_keys[15], 71), 0),
        "head_mask": with_ends((jax.random.randint(arg_keys[6], (HEADS,), 0, 20) < 19).astype(jnp.int32), jax.random.fold_in(arg_keys[6], 1), 0, 1),
        "hidden": normal_values(arg_keys[7], (2, IMG, D), 1.0, 6.0, ((0, 2), (1, 64))),
        "out_weight": normal_values(arg_keys[8], (HD, D), HD ** -0.5, 0.125, ((0, 8),)),
        "out_bias": normal_values(arg_keys[9], (D,), 0.5, 3.0),
        "final_shift": normal_values(arg_keys[10], (2, D), 0.5, 3.0, ((0, 2),)),
        "final_scale": normal_values(arg_keys[11], (2, D), 0.3, 1.5, ((0, 2),)),
        "final_weight": normal_values(arg_keys[12], (CH, D), D ** -0.5, 0.125),
        "latent": normal_values(arg_keys[13], (CH, IMG), 1.0, 6.0, ((0, 2), (1, 64)), jnp.float32),
        "step_index": jax.random.randint(arg_keys[14], (1,), 0, STEPS).astype(jnp.int32),
    }


GUIDANCE = 3.5

def sigma_at(position):
    level = 1.0 - position.astype(jnp.float32) / STEPS
    return 3.0 * level / (1.0 + 2.0 * level)

def attend_head(query_rows, key_rows, value_rows, usable):
    block = math.gcd(IMG, 1024)
    blocks = query_rows.reshape(IMG // block, block, HDIM)

    def one_block(query_block):
        scores = jnp.dot(query_block, key_rows.T, preferred_element_type=jnp.float32) * HDIM ** (-0.5)
        scores = jnp.where(usable[None, :], scores, -1e+30)
        highest = lax.optimization_barrier(jnp.max(scores, axis=1, keepdims=True))
        weights = jnp.exp(scores - highest)
        totals = lax.optimization_barrier(jnp.sum(weights, axis=1, keepdims=True))
        summed = jnp.dot(weights.astype(jnp.bfloat16), value_rows, preferred_element_type=jnp.float32)
        return summed / totals
    return lax.map(one_block, blocks).reshape(IMG, HDIM)

def branch_velocity(b, q_img, k_img, v_img, text_k, text_v, text_len, head_mask, hidden, out_weight, out_bias, final_shift, final_scale, final_weight):
    queries = q_img[b].reshape(IMG, HEADS, HDIM).transpose(1, 0, 2)
    all_keys = jnp.concatenate([k_img[b], text_k[b]], 0).reshape(IMG + TXT, HEADS, HDIM).transpose(1, 0, 2)
    all_values = jnp.concatenate([v_img[b], text_v[b]], 0).reshape(IMG + TXT, HEADS, HDIM).transpose(1, 0, 2)
    usable = jnp.concatenate([jnp.ones((IMG,), dtype=bool), jnp.arange(TXT) < text_len[b]])
    heads_out = lax.map(lambda triple: attend_head(triple[0], triple[1], triple[2], usable), (queries, all_keys, all_values))
    heads_out = (heads_out * head_mask.astype(jnp.float32)[:, None, None]).astype(jnp.bfloat16)
    attended = heads_out.transpose(1, 0, 2).reshape(IMG, HD)
    projected = jnp.dot(attended, out_weight, preferred_element_type=jnp.float32)
    residual = hidden[b].astype(jnp.float32) + projected + out_bias.astype(jnp.float32)
    centre = lax.optimization_barrier(jnp.mean(residual, axis=1, keepdims=True))
    spread = lax.optimization_barrier(jnp.mean((residual - centre) ** 2, axis=1, keepdims=True))
    normed = (residual - centre) / jnp.sqrt(spread + 1e-06)
    modulated = (normed * (1.0 + final_scale[b].astype(jnp.float32)) + final_shift[b].astype(jnp.float32)).astype(jnp.bfloat16)
    return jnp.dot(final_weight, modulated.T, preferred_element_type=jnp.float32)

def reference(q_img, k_img, v_img, text_k, text_v, text_len, head_mask, hidden, out_weight, out_bias, final_shift, final_scale, final_weight, latent, step_index):
    cond_velocity = branch_velocity(0, q_img, k_img, v_img, text_k, text_v, text_len, head_mask, hidden, out_weight, out_bias, final_shift, final_scale, final_weight)
    uncond_velocity = branch_velocity(1, q_img, k_img, v_img, text_k, text_v, text_len, head_mask, hidden, out_weight, out_bias, final_shift, final_scale, final_weight)
    guided = uncond_velocity + GUIDANCE * (cond_velocity - uncond_velocity)
    sigma_now = sigma_at(step_index[0])
    sigma_next = sigma_at(step_index[0] + 1)
    denoised = latent - sigma_now * guided
    next_latent = latent + (sigma_next - sigma_now) * guided
    return (next_latent, denoised)
```

```python
import functools

import jax
import jax.numpy as jnp
from jax import lax
from jax.experimental import pallas as pl
from jax.experimental.pallas import tpu as pltpu
from jax.sharding import PartitionSpec as P

HDIM = 64
STEPS = 28
GUIDANCE = 3.5
GROUP_HEADS = 5
FEATURES = 320
TOKENS = 128
SLOTS = 384
QUERIES = 1024
TILE = 256
SCORE_SCALE = 0.125 * 1.4426950408889634
MESH = pl.DeviceIdType.MESH
f32 = jnp.float32
bf16 = jnp.bfloat16


def sigma_at(position):
    level = 1.0 - position.astype(jnp.float32) / STEPS
    return 3.0 * level / (1.0 + 2.0 * level)


def attention_kernel(
    q_hbm,
    k_hbm,
    v_hbm,
    tk_hbm,
    tv_hbm,
    bias_ref,
    mask_ref,
    o_ref,
    loaded,
    text_slab,
    q_stage,
    kv_stage,
    o_stage,
    q_recv,
    kv,
    qx,
    text_keys,
    text_values,
    s0,
    s1,
    p0,
    p1,
    m_ref,
    acc,
    load_sem,
    q_send,
    q_recv_sem,
    a_send,
    a_recv,
    b_send,
    b_recv,
    o_send,
    o_recv,
):
    seq = lax.axis_index("seq")
    group = lax.axis_index("head")
    core = lax.rem(seq, 2)
    parity = lax.rem(group, 2)
    right = lax.rem(seq + 2, 8)
    left = lax.rem(seq + 6, 8)
    sibling = seq + 1 - 2 * core
    far = lax.rem(seq + 2 + 4 * core, 8)

    slab_start = pl.multiple_of(128 * ((5 * group) // 2), 128)
    loads = [
        pltpu.make_async_copy(src.at[0], loaded.at[i], load_sem.at[i])
        for i, src in enumerate((q_hbm, k_hbm, v_hbm))
    ] + [
        pltpu.make_async_copy(
            src.at[0, :, pl.ds(slab_start, 384)], text_slab.at[i], load_sem.at[3 + i]
        )
        for i, src in enumerate((tk_hbm, tv_hbm))
    ]
    for load in loads:
        load.start()

    barrier = pltpu.get_barrier_semaphore()
    for d in range(1, 8):
        pl.semaphore_signal(
            barrier, inc=1, device_id={"head": lax.rem(group + d, 8)}, device_id_type=MESH
        )
    for near in (right, left, sibling):
        pl.semaphore_signal(barrier, inc=1, device_id={"seq": near}, device_id_type=MESH)

    low = lax.broadcasted_iota(jnp.int32, (TOKENS, 128), 1) < HDIM
    low_half = lax.broadcasted_iota(jnp.int32, (HDIM, 128), 1) < HDIM

    loads[0].wait()
    for i in range(20):
        block = loaded[0, :, 128 * i : 128 * (i + 1)].T
        for half in range(2):
            f = 128 * i + HDIM * half
            q_stage[f // FEATURES, pl.ds(f % FEATURES, HDIM), :] = block[HDIM * half : HDIM * (half + 1)]
    pl.semaphore_wait(barrier, 10)

    def q_copy(d):
        peer = lax.rem(group + d, 8)
        return pltpu.make_async_remote_copy(
            src_ref=q_stage.at[peer],
            dst_ref=q_recv.at[group],
            send_sem=q_send.at[d],
            recv_sem=q_recv_sem.at[d],
            device_id={"head": peer},
            device_id_type=MESH,
        )

    def kv_copy(d):
        peer = lax.rem(group + d, 8)
        return pltpu.make_async_remote_copy(
            src_ref=kv_stage.at[peer],
            dst_ref=kv.at[d % 2, group // 2],
            send_sem=a_send.at[d],
            recv_sem=a_recv.at[d],
            device_id={"head": peer},
            device_id_type=MESH,
        )

    order = (2, 6, 4, 1, 7, 3, 5)
    for d in order:
        q_copy(d).start()
    q_recv[pl.ds(group, 1)] = q_stage[pl.ds(group, 1)]

    loads[1].wait()
    loads[2].wait()
    for p in range(8):
        first = (5 * p) // 2
        tiles = [
            loaded[1, :, 128 * (first + i) : 128 * (first + i + 1)].astype(f32) for i in range(3)
        ]
        if p % 2 == 0:
            kv_stage[p, 0:128, :] = tiles[0].astype(bf16)
            kv_stage[p, 128:256, :] = tiles[1].astype(bf16)
            last = jnp.where(low_half, tiles[2][:HDIM], pltpu.roll(tiles[2][HDIM:], HDIM, 1))
        else:
            kv_stage[p, 0:128, :] = jnp.where(low, tiles[1], tiles[0]).astype(bf16)
            kv_stage[p, 128:256, :] = jnp.where(low, tiles[2], tiles[1]).astype(bf16)
            last = jnp.where(low_half, pltpu.roll(tiles[2][:HDIM], HDIM, 1), tiles[2][HDIM:])
        kv_stage[p, 256:320, :] = last.astype(bf16)
    for i in range(20):
        block = loaded[2, :, 128 * i : 128 * (i + 1)].T
        for half in range(2):
            f = 128 * i + HDIM * half
            kv_stage[f // FEATURES, pl.ds(FEATURES + f % FEATURES, HDIM), :] = block[
                HDIM * half : HDIM * (half + 1)
            ]
    for d in order:
        kv_copy(d).start()
    kv[0, pl.ds(group // 2, 1)] = kv_stage[pl.ds(group, 1)]

    loads[3].wait()
    loads[4].wait()
    odd = parity == 1
    swap = jnp.logical_and(lax.broadcasted_iota(jnp.int32, (SLOTS, 128), 1) < HDIM, odd)
    slabs = [text_slab[0, :, 128 * i : 128 * (i + 1)].astype(f32) for i in range(3)]
    text_keys[0] = jnp.where(swap, slabs[1], slabs[0]).astype(bf16)
    text_keys[1] = jnp.where(swap, slabs[2], slabs[1]).astype(bf16)
    text_keys[2] = slabs[2].astype(bf16)
    for i in range(3):
        for j in range(3):
            text_values[128 * i : 128 * (i + 1), 128 * j : 128 * (j + 1)] = text_slab[
                1, 128 * j : 128 * (j + 1), 128 * i : 128 * (i + 1)
            ].T

    for d in order:
        q_copy(d).wait_recv()
    zero = jnp.zeros((HDIM, TILE), bf16)

    def place(t, _):
        for h in range(GROUP_HEADS):
            q = jnp.concatenate(
                [q_recv[2 * t, HDIM * h : HDIM * (h + 1)], q_recv[2 * t + 1, HDIM * h : HDIM * (h + 1)]], 1
            )
            if h < 4:
                offset = parity if h % 2 == 0 else 1 - parity
                qx[6 * t + h, pl.ds(pl.multiple_of(HDIM * offset, HDIM), HDIM), :] = q
                qx[6 * t + h, pl.ds(pl.multiple_of(HDIM * (1 - offset), HDIM), HDIM), :] = zero
            else:
                for side in range(2):
                    qx[6 * t + 4 + side, HDIM * side : HDIM * (side + 1), :] = q
                    qx[6 * t + 4 + side, HDIM * (1 - side) : HDIM * (2 - side), :] = zero
        return 0

    lax.fori_loop(0, 4, place, 0)

    ones = jnp.ones((16, 512), bf16)

    def text_units(t, _):
        for h in range(GROUP_HEADS):
            weights_at = 6 * t + h if h < 4 else 6 * t + 4 + parity
            s = jnp.dot(text_keys[h // 2], qx[weights_at], preferred_element_type=f32) + bias_ref[...]
            top = jnp.max(s, axis=0, keepdims=True)
            p = jnp.exp2((s - top) * SCORE_SCALE).astype(bf16)
            values = text_values[pl.ds(pl.multiple_of(HDIM * (parity + h), HDIM), HDIM), :]
            acc[GROUP_HEADS * t + h] = jnp.dot(
                jnp.concatenate([values, ones[:, :SLOTS]], 0), p, preferred_element_type=f32
            )
            m_ref[GROUP_HEADS * t + h] = top
        return 0

    lax.fori_loop(0, 4, text_units, 0)

    def ring_copy(k, src, dst, target):
        return pltpu.make_async_remote_copy(
            src_ref=kv.at[src],
            dst_ref=kv.at[dst],
            send_sem=b_send.at[k],
            recv_sem=b_recv.at[dst],
            device_id={"seq": target},
            device_id_type=MESH,
        )

    copies = {
        0: (ring_copy(0, 0, 4, right), ring_copy(1, 0, 5, left), ring_copy(2, 0, 2, sibling)),
        1: (ring_copy(3, 1, 8, right), ring_copy(4, 1, 9, left), ring_copy(5, 1, 3, sibling)),
        2: (ring_copy(6, 4 + core, 12, far), ring_copy(7, 4, 6, sibling), ring_copy(8, 5, 7, sibling)),
        3: (ring_copy(9, 8 + core, 14, far), ring_copy(10, 8, 10, sibling), ring_copy(11, 9, 11, sibling)),
        4: (ring_copy(12, 12, 13, sibling),),
        5: (ring_copy(13, 14, 15, sibling),),
    }

    def arrived(dst):
        ring_copy(0, dst, dst, sibling).wait_recv()

    def send(stage):
        for copy in copies[stage]:
            copy.start()

    for d in (2, 6, 4):
        kv_copy(d).wait_recv()
    send(0)
    for d in (1, 7, 3, 5):
        kv_copy(d).wait_recv()
    send(1)

    s_bufs = (s0, s1)
    p_bufs = (p0, p1)

    def scores(step, r, h, buf):
        t = r // GROUP_HEADS
        best = None
        for side in range(2):
            slot = 2 * step + side
            if h < 4:
                lhs = jnp.concatenate(
                    [kv[slot, b, 128 * (h // 2) : 128 * (h // 2 + 1), :] for b in range(4)], 0
                )
                s = jnp.dot(lhs, qx[6 * t + h], preferred_element_type=f32)
                buf[512 * side : 512 * (side + 1), :] = s
                top = jnp.max(s.reshape(64, 8, TILE), axis=0)
                best = top if best is None else jnp.maximum(best, top)
            else:
                lhs = jnp.concatenate([kv[slot, b, 256:320, :] for b in range(4)], 0)
                for half in range(2):
                    s = jnp.dot(lhs, qx[6 * t + 4 + half], preferred_element_type=f32)
                    for b in range(4):
                        at = 512 * side + 128 * b + HDIM * half
                        buf[at : at + HDIM, :] = s[HDIM * b : HDIM * (b + 1)]
                    top = jnp.max(s.reshape(32, 8, TILE), axis=0)
                    best = top if best is None else jnp.maximum(best, top)
        old = m_ref[r]
        new = jnp.maximum(old, jnp.max(best, axis=0, keepdims=True))
        m_ref[r] = new
        return new, jnp.exp2((old - new) * SCORE_SCALE)

    def weigh(buf, top, out):
        for j in range(4):
            rows = slice(256 * j, 256 * (j + 1))
            out[rows, :] = jnp.exp2((buf[rows, :] - top) * SCORE_SCALE).astype(bf16)

    def add_values(step, r, h, rescale, buf):
        total = None
        for side in range(2):
            slot = 2 * step + side
            rows = FEATURES + HDIM * h
            lhs = jnp.concatenate([kv[slot, b, rows : rows + HDIM, :] for b in range(4)], 1)
            part = jnp.dot(
                jnp.concatenate([lhs, ones], 0),
                buf[512 * side : 512 * (side + 1), :],
                preferred_element_type=f32,
            )
            total = part if total is None else total + part
        acc[r] = acc[r] * rescale + total

    def one_step(step, _):
        @pl.when(step == 1)
        def _():
            arrived(2)
            arrived(3)

        @pl.when(step == 2)
        def _():
            arrived(4)
            arrived(5)
            send(2)

        @pl.when(step == 3)
        def _():
            arrived(6)
            arrived(7)

        @pl.when(step == 4)
        def _():
            arrived(8)
            arrived(9)
            send(3)

        @pl.when(step == 5)
        def _():
            arrived(10)
            arrived(11)

        @pl.when(step == 6)
        def _():
            arrived(12)
            send(4)
            arrived(13)

        @pl.when(step == 7)
        def _():
            arrived(14)
            send(5)
            arrived(15)

        p1[...] = jnp.zeros_like(p1)
        top, rescale = scores(step, 0, 0, s0)

        def ten(i, carry):
            top, rescale, before = carry
            for j in range(10):
                r = 10 * i + j
                last_r = jnp.maximum(r - 1, 0)
                next_r = lax.rem(r + 1, 20)
                add_values(step, last_r, (j - 1) % 5, before, p_bufs[(j + 1) % 2])
                weigh(s_bufs[j % 2], top, p_bufs[j % 2])
                if j < 9:
                    following = scores(step, r + 1, (j + 1) % 5, s_bufs[(j + 1) % 2])
                else:
                    following = scores(step, next_r, 0, s_bufs[0])
                before = rescale
                top, rescale = following
            return top, rescale, before

        top, rescale, before = lax.fori_loop(0, 2, ten, (top, rescale, jnp.ones_like(top)))
        add_values(step, 19, 4, before, p1)
        return 0

    lax.fori_loop(0, 8, one_step, 0)

    def finish(t, _):
        for h in range(GROUP_HEADS):
            sums = acc[GROUP_HEADS * t + h]
            gain = mask_ref[GROUP_HEADS * group + h].astype(f32)
            out = (sums[:HDIM] / sums[HDIM : HDIM + 1] * gain).astype(bf16)
            o_stage[2 * t, HDIM * h : HDIM * (h + 1), :] = out[:, :128]
            o_stage[2 * t + 1, HDIM * h : HDIM * (h + 1), :] = out[:, 128:]
        return 0

    lax.fori_loop(0, 4, finish, 0)

    def o_copy(d):
        peer = lax.rem(group + d, 8)
        return pltpu.make_async_remote_copy(
            src_ref=o_stage.at[peer],
            dst_ref=o_ref.at[group],
            send_sem=o_send.at[d],
            recv_sem=o_recv.at[d],
            device_id={"head": peer},
            device_id_type=MESH,
        )

    for d in order:
        o_copy(d).start()
    o_ref[pl.ds(group, 1)] = o_stage[pl.ds(group, 1)]
    for d in order:
        q_copy(d).wait_send()
        kv_copy(d).wait_send()
    for stage in copies.values():
        for copy in stage:
            copy.wait_send()
    for d in order:
        o_copy(d).wait_recv()
        o_copy(d).wait_send()


def attend(q, k, v, text_k, text_v, bias, head_mask):
    vmem = functools.partial(pltpu.VMEM)
    dma = pltpu.SemaphoreType.DMA
    anywhere = pl.BlockSpec(memory_space=pl.ANY)
    return pl.pallas_call(
        attention_kernel,
        out_shape=jax.ShapeDtypeStruct((8, FEATURES, TOKENS), bf16),
        in_specs=[anywhere] * 5
        + [pl.BlockSpec(memory_space=pltpu.VMEM), pl.BlockSpec(memory_space=pltpu.SMEM)],
        out_specs=pl.BlockSpec(memory_space=pltpu.VMEM),
        scratch_shapes=[
            vmem((3, TOKENS, 2560), bf16),
            vmem((2, SLOTS, 384), bf16),
            vmem((8, FEATURES, TOKENS), bf16),
            vmem((8, 2 * FEATURES, TOKENS), bf16),
            vmem((8, FEATURES, TOKENS), bf16),
            vmem((8, FEATURES, TOKENS), bf16),
            vmem((16, 4, 2 * FEATURES, TOKENS), bf16),
            vmem((24, 128, TILE), bf16),
            vmem((3, SLOTS, 128), bf16),
            vmem((384, SLOTS), bf16),
            vmem((QUERIES, TILE), f32),
            vmem((QUERIES, TILE), f32),
            vmem((QUERIES, TILE), bf16),
            vmem((QUERIES, TILE), bf16),
            vmem((20, 1, TILE), f32),
            vmem((20, 80, TILE), f32),
            dma((5,)),
            dma((8,)),
            dma((8,)),
            dma((8,)),
            dma((8,)),
            dma((14,)),
            dma((16,)),
            dma((8,)),
            dma((8,)),
        ],
        compiler_params=pltpu.CompilerParams(
            collective_id=0, has_side_effects=True, vmem_limit_bytes=48 << 20
        ),
        cost_estimate=pl.CostEstimate(
            flops=40_000_000_000, bytes_accessed=8_000_000, transcendentals=44_000_000
        ),
    )(q, k, v, text_k, text_v, bias, head_mask)


def gather_weight(out_weight):
    core = lax.axis_index("seq") % 2
    rows = out_weight.shape[0] // 2
    mine = lax.dynamic_slice_in_dim(out_weight, core * rows, rows, 0)
    mine = lax.all_gather(mine, "head", axis=0, tiled=False)
    other = lax.ppermute(mine, "seq", [(i, i ^ 1) for i in range(8)])
    first = jnp.where(core == 0, mine, other)
    second = jnp.where(core == 0, other, mine)
    return jnp.stack([first, second], 1).reshape(-1, out_weight.shape[1])


def shards(
    q_img,
    k_img,
    v_img,
    text_k,
    text_v,
    text_len,
    head_mask,
    hidden,
    out_weight,
    out_bias,
    final_shift,
    final_scale,
    final_weight,
    latent,
    step_index,
):
    live = jnp.arange(SLOTS) < text_len[0]
    bias = jnp.broadcast_to(jnp.where(live, 0.0, -1e30).astype(f32)[:, None], (SLOTS, TILE))
    attended = attend(q_img, k_img, v_img, text_k, text_v, bias, head_mask)
    attended = attended.reshape(8 * FEATURES, TOKENS)
    own_rows = hidden.shape[1]
    projected = lax.dot_general(
        attended,
        lax.all_gather(out_weight, "head", axis=0, tiled=True),
        (((0,), (0,)), ((), ())),
        preferred_element_type=jnp.float32,
    )
    residual = hidden[0].astype(jnp.float32) + projected + out_bias.astype(jnp.float32)
    centre = jnp.mean(residual, axis=1, keepdims=True)
    spread = jnp.mean((residual - centre) ** 2, axis=1, keepdims=True)
    normed = (residual - centre) / jnp.sqrt(spread + 1e-06)
    modulated = (
        normed * (1.0 + final_scale[0].astype(jnp.float32)) + final_shift[0].astype(jnp.float32)
    ).astype(jnp.bfloat16)
    velocity = jnp.einsum("cd,td->ct", final_weight, modulated, preferred_element_type=jnp.float32)
    channel_half = velocity.shape[0] // 2
    halves = velocity.reshape(2, 1, channel_half, own_rows)
    branches = lax.all_to_all(
        halves.astype(jnp.bfloat16), "cfg", split_axis=0, concat_axis=1, tiled=True
    ).astype(halves.dtype)
    cond_velocity = branches[0, 0]
    uncond_velocity = branches[0, 1]
    guided = uncond_velocity + GUIDANCE * (cond_velocity - uncond_velocity)
    sigma_now = sigma_at(step_index[0])
    sigma_next = sigma_at(step_index[0] + 1)
    denoised = latent - sigma_now * guided
    next_latent = latent + (sigma_next - sigma_now) * guided
    return (next_latent, denoised)


def solution(mesh):
    in_specs = (
        P("cfg", ("seq", "head"), None),
        P("cfg", ("seq", "head"), None),
        P("cfg", ("seq", "head"), None),
        P("cfg", None, None),
        P("cfg", None, None),
        P("cfg"),
        P(),
        P("cfg", ("seq", "head"), None),
        P("head", None),
        P(),
        P("cfg", None),
        P("cfg", None),
        P(),
        P("cfg", ("seq", "head")),
        P(),
    )
    out_specs = (P("cfg", ("seq", "head")), P("cfg", ("seq", "head")))
    return jax.shard_map(shards, mesh=mesh, in_specs=in_specs, out_specs=out_specs, check_vma=False)
```

```python
import functools

import jax
import jax.numpy as jnp
from jax import lax
from jax.experimental import pallas as pl
from jax.experimental.pallas import tpu as pltpu
from jax.sharding import PartitionSpec as P

HDIM = 64
STEPS = 28
GUIDANCE = 3.5
GROUP_HEADS = 5
FEATURES = 320
TOKENS = 128
SLOTS = 384
QUERIES = 1024
TILE = 256
SCORE_SCALE = 0.125 * 1.4426950408889634
MESH = pl.DeviceIdType.MESH
f32 = jnp.float32
bf16 = jnp.bfloat16


def sigma_at(position):
    level = 1.0 - position.astype(jnp.float32) / STEPS
    return 3.0 * level / (1.0 + 2.0 * level)


def block_kernel(
    q_hbm,
    k_hbm,
    v_hbm,
    tk_hbm,
    tv_hbm,
    w_hbm,
    hidden_hbm,
    len_ref,
    mask_ref,
    step_ref,
    out_bias,
    shift_ref,
    scale_ref,
    final_weight,
    latent_ref,
    next_ref,
    denoised_ref,
    loaded,
    text_slab,
    q_stage,
    kv_stage,
    o_stage,
    q_recv,
    o_recv,
    kv,
    weight,
    qx,
    text_keys,
    text_values,
    s0,
    s1,
    p0,
    p1,
    m_ref,
    acc,
    hidden,
    attended,
    residual,
    v_stage,
    v_recv,
    load_sem,
    q_send,
    q_recv_sem,
    a_send,
    a_recv,
    b_send,
    b_recv,
    o_send,
    o_recv_sem,
    w_send,
    w_recv,
    v_sem,
):
    cfg = lax.axis_index("cfg")
    seq = lax.axis_index("seq")
    group = lax.axis_index("head")
    core = lax.rem(seq, 2)
    parity = lax.rem(group, 2)
    row = group // 2
    right = lax.rem(seq + 2, 8)
    left = lax.rem(seq + 6, 8)
    sibling = seq + 1 - 2 * core
    far = lax.rem(seq + 2 + 4 * core, 8)
    turned = group + 1 - 2 * parity
    w_right = lax.rem(group + 2, 8)
    w_left = lax.rem(group + 6, 8)
    w_opposite = lax.rem(group + 4, 8)
    w_far = lax.rem(group + 2 + 4 * core, 8)

    slab_start = pl.multiple_of(128 * ((5 * group) // 2), 128)
    loads = (
        [
            pltpu.make_async_copy(src.at[0], loaded.at[i], load_sem.at[i])
            for i, src in enumerate((q_hbm, k_hbm, v_hbm))
        ]
        + [
            pltpu.make_async_copy(
                src.at[0, :, pl.ds(slab_start, 384)], text_slab.at[i], load_sem.at[3 + i]
            )
            for i, src in enumerate((tk_hbm, tv_hbm))
        ]
        + [
            pltpu.make_async_copy(
                w_hbm.at[pl.ds(160 * i, 160)], weight.at[2 * group + i], load_sem.at[5 + i]
            )
            for i in range(2)
        ]
        + [pltpu.make_async_copy(hidden_hbm.at[0], hidden, load_sem.at[7])]
    )
    for load in loads:
        load.start()

    barrier = pltpu.get_barrier_semaphore()
    for d in range(1, 8):
        pl.semaphore_signal(
            barrier, inc=1, device_id={"head": lax.rem(group + d, 8)}, device_id_type=MESH
        )
    for near in (right, left, sibling):
        pl.semaphore_signal(barrier, inc=1, device_id={"seq": near}, device_id_type=MESH)
    pl.semaphore_signal(barrier, inc=1, device_id={"cfg": 1 - cfg}, device_id_type=MESH)
    pl.semaphore_signal(
        barrier, inc=1, device_id={"cfg": 1 - cfg, "head": turned}, device_id_type=MESH
    )

    low = lax.broadcasted_iota(jnp.int32, (TOKENS, 128), 1) < HDIM
    low_half = lax.broadcasted_iota(jnp.int32, (HDIM, 128), 1) < HDIM

    loads[0].wait()
    for i in range(20):
        block = loaded[0, :, 128 * i : 128 * (i + 1)].T
        for half in range(2):
            f = 128 * i + HDIM * half
            q_stage[f // FEATURES, pl.ds(f % FEATURES, HDIM), :] = block[
                HDIM * half : HDIM * (half + 1)
            ]
    pl.semaphore_wait(barrier, 12)

    def head_copy(src, dst, send, recv, d):
        peer = lax.rem(group + d, 8)
        return pltpu.make_async_remote_copy(
            src_ref=src.at[peer],
            dst_ref=dst.at[d % 2, row],
            send_sem=send.at[d],
            recv_sem=recv.at[d],
            device_id={"head": peer},
            device_id_type=MESH,
        )

    def q_copy(d):
        return head_copy(q_stage, q_recv, q_send, q_recv_sem, d)

    def kv_copy(d):
        return head_copy(kv_stage, kv, a_send, a_recv, d)

    along = (2, 6, 4)
    across = (1, 7, 3, 5)
    for d in along:
        q_copy(d).start()
    q_recv[0, pl.ds(row, 1)] = q_stage[pl.ds(group, 1)]

    loads[1].wait()
    loads[2].wait()
    for p in range(8):
        first = (5 * p) // 2
        tiles = [
            loaded[1, :, 128 * (first + i) : 128 * (first + i + 1)].astype(f32) for i in range(3)
        ]
        if p % 2 == 0:
            kv_stage[p, 0:128, :] = tiles[0].astype(bf16)
            kv_stage[p, 128:256, :] = tiles[1].astype(bf16)
            last = jnp.where(low_half, tiles[2][:HDIM], pltpu.roll(tiles[2][HDIM:], HDIM, 1))
        else:
            kv_stage[p, 0:128, :] = jnp.where(low, tiles[1], tiles[0]).astype(bf16)
            kv_stage[p, 128:256, :] = jnp.where(low, tiles[2], tiles[1]).astype(bf16)
            last = jnp.where(low_half, pltpu.roll(tiles[2][:HDIM], HDIM, 1), tiles[2][HDIM:])
        kv_stage[p, 256:320, :] = last.astype(bf16)
    for i in range(20):
        block = loaded[2, :, 128 * i : 128 * (i + 1)].T
        for half in range(2):
            f = 128 * i + HDIM * half
            kv_stage[f // FEATURES, pl.ds(FEATURES + f % FEATURES, HDIM), :] = block[
                HDIM * half : HDIM * (half + 1)
            ]
    for d in along:
        kv_copy(d).start()
    for d in across:
        q_copy(d).start()
    for d in across:
        kv_copy(d).start()
    kv[0, pl.ds(row, 1)] = kv_stage[pl.ds(group, 1)]

    loads[3].wait()
    loads[4].wait()
    odd = parity == 1
    swap = jnp.logical_and(lax.broadcasted_iota(jnp.int32, (SLOTS, 128), 1) < HDIM, odd)
    slabs = [text_slab[0, :, 128 * i : 128 * (i + 1)].astype(f32) for i in range(3)]
    text_keys[0] = jnp.where(swap, slabs[1], slabs[0]).astype(bf16)
    text_keys[1] = jnp.where(swap, slabs[2], slabs[1]).astype(bf16)
    text_keys[2] = slabs[2].astype(bf16)
    for i in range(3):
        for j in range(3):
            text_values[128 * i : 128 * (i + 1), 128 * j : 128 * (j + 1)] = text_slab[
                1, 128 * j : 128 * (j + 1), 128 * i : 128 * (i + 1)
            ].T

    zero = jnp.zeros((HDIM, TILE), bf16)
    ones = jnp.ones((16, 512), bf16)

    def queries_and_text(t, _):
        dead = lax.broadcasted_iota(jnp.int32, (SLOTS, TILE), 0) >= len_ref[0]
        for h in range(GROUP_HEADS):
            rows = slice(HDIM * h, HDIM * (h + 1))
            q = jnp.concatenate(
                [q_recv[t // 2, 2 * (t % 2), rows], q_recv[t // 2, 2 * (t % 2) + 1, rows]], 1
            )
            if h < 4:
                offset = parity if h % 2 == 0 else 1 - parity
                qx[6 * t + h, pl.ds(pl.multiple_of(HDIM * offset, HDIM), HDIM), :] = q
                qx[6 * t + h, pl.ds(pl.multiple_of(HDIM * (1 - offset), HDIM), HDIM), :] = zero
            else:
                for side in range(2):
                    qx[6 * t + 4 + side, HDIM * side : HDIM * (side + 1), :] = q
                    qx[6 * t + 4 + side, HDIM * (1 - side) : HDIM * (2 - side), :] = zero
        for h in range(GROUP_HEADS):
            weights_at = 6 * t + h if h < 4 else 6 * t + 4 + parity
            s = jnp.dot(text_keys[h // 2], qx[weights_at], preferred_element_type=f32)
            s = jnp.where(dead, -1e30, s)
            top = jnp.max(s, axis=0, keepdims=True)
            p = jnp.exp2((s - top) * SCORE_SCALE).astype(bf16)
            values = text_values[pl.ds(pl.multiple_of(HDIM * (parity + h), HDIM), HDIM), :]
            acc[GROUP_HEADS * t + h] = jnp.dot(
                jnp.concatenate([values, ones[:, :SLOTS]], 0), p, preferred_element_type=f32
            )
            m_ref[GROUP_HEADS * t + h] = top
        return 0

    for d in along:
        q_copy(d).wait_recv()
    lax.fori_loop(0, 2, queries_and_text, 0)

    def ring_copy(k, src, dst, target):
        return pltpu.make_async_remote_copy(
            src_ref=kv.at[src],
            dst_ref=kv.at[dst],
            send_sem=b_send.at[k],
            recv_sem=b_recv.at[dst],
            device_id={"seq": target},
            device_id_type=MESH,
        )

    copies = {
        0: (ring_copy(2, 0, 2, sibling), ring_copy(0, 0, 4, right), ring_copy(1, 0, 5, left)),
        1: (ring_copy(5, 1, 3, sibling), ring_copy(3, 1, 8, right), ring_copy(4, 1, 9, left)),
        2: (ring_copy(6, 4 + core, 12, far), ring_copy(7, 4, 6, sibling), ring_copy(8, 5, 7, sibling)),
        3: (ring_copy(9, 8 + core, 14, far), ring_copy(10, 8, 10, sibling), ring_copy(11, 9, 11, sibling)),
        4: (ring_copy(12, 12, 13, sibling),),
        5: (ring_copy(13, 14, 15, sibling),),
    }

    def arrived(*slots):
        for dst in slots:
            ring_copy(0, dst, dst, sibling).wait_recv()

    def send(stage):
        for copy in copies[stage]:
            copy.start()

    def weight_copy(k, owner, target, from_hbm=False):
        at = 2 * owner + core
        return pltpu.make_async_remote_copy(
            src_ref=w_hbm.at[pl.ds(pl.multiple_of(160 * core, 160), 160)] if from_hbm else weight.at[at],
            dst_ref=weight.at[at],
            send_sem=w_send.at[k],
            recv_sem=w_recv.at[k],
            device_id=target,
            device_id_type=MESH,
        )

    to_right, to_left = {"head": w_right}, {"head": w_left}
    to_turned = {"cfg": 1 - cfg, "head": turned}
    to_sibling = {"seq": sibling}
    owners = (
        w_left,
        w_right,
        turned,
        w_opposite,
        lax.rem(turned + 6, 8),
        lax.rem(turned + 2, 8),
        lax.rem(turned + 4, 8),
    )
    weight_copies = {
        0: (
            weight_copy(0, group, to_right, True),
            weight_copy(1, group, to_left, True),
            weight_copy(2, group, to_turned, True),
        ),
        1: (
            weight_copy(3, lax.rem(group + 6 + 4 * core, 8), {"head": w_far}),
            weight_copy(4, turned, to_right),
            weight_copy(5, turned, to_left),
        ),
        2: (weight_copy(6, w_opposite, to_turned),),
    }
    to_core = [weight_copy(7 + k, owners[k], to_sibling) for k in range(7)]

    def weight_arrived(*which):
        for k in which:
            weight_copy(k, group, to_sibling).wait_recv()

    def weight_send(stage):
        for copy in weight_copies[stage]:
            copy.start()

    def share(*which):
        for k in which:
            to_core[k].start()

    s_bufs = (s0, s1)
    p_bufs = (p0, p1)

    def scores(step, r, t, h, buf):
        best = None
        for side in range(2):
            slot = step[side]
            if h < 4:
                lhs = jnp.concatenate(
                    [kv[slot, b, 128 * (h // 2) : 128 * (h // 2 + 1), :] for b in range(4)], 0
                )
                s = jnp.dot(lhs, qx[6 * t + h], preferred_element_type=f32)
                buf[512 * side : 512 * (side + 1), :] = s
                top = jnp.max(s.reshape(64, 8, TILE), axis=0)
                best = top if best is None else jnp.maximum(best, top)
            else:
                lhs = jnp.concatenate([kv[slot, b, 256:320, :] for b in range(4)], 0)
                for half in range(2):
                    s = jnp.dot(lhs, qx[6 * t + 4 + half], preferred_element_type=f32)
                    for b in range(4):
                        at = 512 * side + 128 * b + HDIM * half
                        buf[at : at + HDIM, :] = s[HDIM * b : HDIM * (b + 1)]
                    top = jnp.max(s.reshape(32, 8, TILE), axis=0)
                    best = top if best is None else jnp.maximum(best, top)
        old = m_ref[r]
        new = jnp.maximum(old, jnp.max(best, axis=0, keepdims=True))
        m_ref[r] = new
        return new, jnp.exp2((old - new) * SCORE_SCALE)

    def weigh(buf, top, out):
        for j in range(4):
            rows = slice(256 * j, 256 * (j + 1))
            out[rows, :] = jnp.exp2((buf[rows, :] - top) * SCORE_SCALE).astype(bf16)

    def add_values(step, r, h, rescale, buf):
        total = None
        for side in range(2):
            slot = step[side]
            rows = FEATURES + HDIM * h
            lhs = jnp.concatenate([kv[slot, b, rows : rows + HDIM, :] for b in range(4)], 1)
            part = jnp.dot(
                jnp.concatenate([lhs, ones], 0),
                buf[512 * side : 512 * (side + 1), :],
                preferred_element_type=f32,
            )
            total = part if total is None else total + part
        acc[r] = acc[r] * rescale + total

    def finish(t, _):
        for h in range(GROUP_HEADS):
            sums = acc[GROUP_HEADS * t + h]
            gain = mask_ref[GROUP_HEADS * group + h].astype(f32)
            out = (sums[:HDIM] / sums[HDIM : HDIM + 1] * gain).astype(bf16)
            for side in range(2):
                o_stage[t // 2, 2 * (t % 2) + side, HDIM * h : HDIM * (h + 1), :] = out[
                    :, 128 * side : 128 * (side + 1)
                ]
        return 0

    def o_copy(d):
        peer = lax.rem(group + d, 8)
        return pltpu.make_async_remote_copy(
            src_ref=o_stage.at[d % 2, peer // 2],
            dst_ref=o_recv.at[group],
            send_sem=o_send.at[d],
            recv_sem=o_recv_sem.at[d],
            device_id={"head": peer},
            device_id_type=MESH,
        )

    def at_start(half):
        @pl.when(half == 0)
        def _():
            for d in along:
                kv_copy(d).wait_recv()
            send(0)
            arrived(2)

        @pl.when(half == 1)
        def _():
            for d in across:
                q_copy(d).wait_recv()
            lax.fori_loop(2, 4, queries_and_text, 0)

        @pl.when(half == 2)
        def _():
            for d in across:
                kv_copy(d).wait_recv()
            send(1)
            weight_send(0)
            arrived(3)

        @pl.when(half == 4)
        def _():
            arrived(4, 5)
            send(2)

        @pl.when(half == 6)
        def _():
            arrived(6, 7)

        @pl.when(half == 7)
        def _():
            arrived(12)
            send(4)

        @pl.when(half == 8)
        def _():
            arrived(13)
            weight_arrived(0, 1, 2)
            weight_send(1)
            share(0, 1, 2)

        @pl.when(half == 10)
        def _():
            arrived(8, 9)
            send(3)

        @pl.when(half == 11)
        def _():
            weight_arrived(3)
            weight_send(2)
            share(3)

        @pl.when(half == 12)
        def _():
            arrived(10, 11)

        @pl.when(half == 13)
        def _():
            arrived(14)
            send(5)

        @pl.when(half == 14)
        def _():
            arrived(15)

        @pl.when(half == 15)
        def _():
            lax.fori_loop(2, 4, finish, 0)
            for d in across:
                o_copy(d).start()

    def half_step(half, _):
        at_start(half)
        order = half // 2
        slots = (
            jnp.where(order == 0, 0, jnp.where(order == 1, 1, 0)),
            jnp.where(order == 0, 2, jnp.where(order == 1, 3, 0)),
        )
        pair = jnp.where(
            order < 4, order, jnp.where(order == 4, 6, jnp.where(order < 7, order - 1, 7))
        )
        one = jnp.where(order < 2, slots[0], 2 * pair)
        two = jnp.where(order < 2, slots[1], 2 * pair + 1)
        side = jnp.where(order == 7, 1 - half % 2, half % 2)
        where = (one, two)

        def unit(j):
            return 10 * side + j, 2 * side + j // 5, j % 5

        top, rescale = scores(where, *unit(0), s0)
        before = None
        for j in range(10):
            if j > 0:
                r, t, h = unit(j - 1)
                add_values(where, r, h, before, p_bufs[(j + 1) % 2])
            weigh(s_bufs[j % 2], top, p_bufs[j % 2])
            before = rescale
            if j < 9:
                top, rescale = scores(where, *unit(j + 1), s_bufs[(j + 1) % 2])
        r, t, h = unit(9)
        add_values(where, r, h, before, p1)
        return 0

    lax.fori_loop(0, 16, half_step, 0)

    lax.fori_loop(0, 2, finish, 0)
    for d in along:
        o_copy(d).start()
    weight_arrived(4, 5, 6)
    share(4, 5, 6)
    o_recv[pl.ds(group, 1)] = o_stage[0, pl.ds(row, 1)]

    for d in along + across:
        q_copy(d).wait_send()
        kv_copy(d).wait_send()
    for stage in copies.values():
        for copy in stage:
            copy.wait_send()
    for stage in weight_copies.values():
        for copy in stage:
            copy.wait_send()

    for d in across + along:
        o_copy(d).wait_recv()
    for p in range(8):
        for h in range(GROUP_HEADS):
            f = FEATURES * p + HDIM * h
            if f % 128 == 0:
                q = f // 128
                lo = o_recv[p, HDIM * h : HDIM * (h + 1), :]
                nxt = f + HDIM
                hi = o_recv[nxt // FEATURES, nxt % FEATURES : nxt % FEATURES + HDIM, :]
                attended[:, 128 * q : 128 * (q + 1)] = jnp.concatenate([lo, hi], 0).T
    for load in loads[5:]:
        load.wait()
    weight_arrived(7, 8, 9, 10, 11, 12, 13)
    rows = attended[...]
    width = 2432
    total = None
    for n in range(0, width, TILE):
        cols = slice(n, min(n + TILE, width))
        part = jnp.dot(
            rows,
            jnp.concatenate([weight[i, :, cols] for i in range(16)], 0),
            preferred_element_type=f32,
        )
        part = hidden[:, cols].astype(f32) + part + out_bias[:, cols].astype(f32)
        residual[:, cols] = part
        part = jnp.sum(part, axis=1, keepdims=True)
        total = part if total is None else total + part
    centre = total / width
    total = None
    for n in range(0, width, TILE):
        cols = slice(n, min(n + TILE, width))
        part = residual[:, cols] - centre
        residual[:, cols] = part
        part = jnp.sum(part * part, axis=1, keepdims=True)
        total = part if total is None else total + part
    norm = 1.0 / jnp.sqrt(total / width + 1e-06)
    velocity = None
    for n in range(0, width, TILE):
        cols = slice(n, min(n + TILE, width))
        modulated = residual[:, cols] * norm * (1.0 + scale_ref[:, cols].astype(f32)) + shift_ref[
            :, cols
        ].astype(f32)
        part = lax.dot_general(
            final_weight[:, cols],
            modulated.astype(bf16),
            (((1,), (1,)), ((), ())),
            preferred_element_type=f32,
        )
        velocity = part if velocity is None else velocity + part
    v_stage[0] = velocity[:32].astype(bf16)
    v_stage[1] = velocity[32:].astype(bf16)
    exchange = pltpu.make_async_remote_copy(
        src_ref=v_stage.at[1 - cfg],
        dst_ref=v_recv,
        send_sem=v_sem.at[0],
        recv_sem=v_sem.at[1],
        device_id={"cfg": 1 - cfg},
        device_id_type=MESH,
    )
    exchange.start()
    mine = jnp.where(cfg == 0, velocity[:32], velocity[32:])
    position = jnp.full((32, TOKENS), step_ref[0], jnp.int32)
    sigma_now = sigma_at(position)
    sigma_next = sigma_at(position + 1)
    for d in along + across:
        o_copy(d).wait_send()
    for copy in to_core:
        copy.wait_send()
    exchange.wait()
    theirs = v_recv[...].astype(f32)
    cond = jnp.where(cfg == 0, mine, theirs)
    uncond = jnp.where(cfg == 0, theirs, mine)
    guided = uncond + GUIDANCE * (cond - uncond)
    denoised_ref[...] = latent_ref[...] - sigma_now * guided
    next_ref[...] = latent_ref[...] + (sigma_next - sigma_now) * guided


def shards(
    q_img,
    k_img,
    v_img,
    text_k,
    text_v,
    text_len,
    head_mask,
    hidden,
    out_weight,
    out_bias,
    final_shift,
    final_scale,
    final_weight,
    latent,
    step_index,
):
    vmem = pltpu.VMEM
    dma = pltpu.SemaphoreType.DMA
    anywhere = pl.BlockSpec(memory_space=pl.ANY)
    scalars = pl.BlockSpec(memory_space=pltpu.SMEM)
    whole = pl.BlockSpec(memory_space=pltpu.VMEM)
    out = jax.ShapeDtypeStruct(latent.shape, f32)
    return pl.pallas_call(
        block_kernel,
        out_shape=(out, out),
        in_specs=[anywhere] * 7 + [scalars] * 3 + [whole] * 5,
        out_specs=(whole, whole),
        scratch_shapes=[
            vmem((3, TOKENS, 2560), bf16),
            vmem((2, SLOTS, 384), bf16),
            vmem((8, FEATURES, TOKENS), bf16),
            vmem((8, 2 * FEATURES, TOKENS), bf16),
            vmem((2, 4, FEATURES, TOKENS), bf16),
            vmem((2, 4, FEATURES, TOKENS), bf16),
            vmem((8, FEATURES, TOKENS), bf16),
            vmem((16, 4, 2 * FEATURES, TOKENS), bf16),
            vmem((16, 160, 2432), bf16),
            vmem((24, 128, TILE), bf16),
            vmem((3, SLOTS, 128), bf16),
            vmem((384, SLOTS), bf16),
            vmem((QUERIES, TILE), f32),
            vmem((QUERIES, TILE), f32),
            vmem((QUERIES, TILE), bf16),
            vmem((QUERIES, TILE), bf16),
            vmem((20, 1, TILE), f32),
            vmem((20, 80, TILE), f32),
            vmem((TOKENS, 2432), bf16),
            vmem((TOKENS, 2560), bf16),
            vmem((TOKENS, 2432), f32),
            vmem((2, 32, TOKENS), bf16),
            vmem((32, TOKENS), bf16),
            dma((8,)),
            dma((8,)),
            dma((8,)),
            dma((8,)),
            dma((8,)),
            dma((14,)),
            dma((16,)),
            dma((8,)),
            dma((8,)),
            dma((14,)),
            dma((14,)),
            dma((2,)),
        ],
        compiler_params=pltpu.CompilerParams(
            collective_id=0, has_side_effects=True, vmem_limit_bytes=60 << 20
        ),
        cost_estimate=pl.CostEstimate(
            flops=40_000_000_000, bytes_accessed=20_000_000, transcendentals=44_000_000
        ),
    )(
        q_img,
        k_img,
        v_img,
        text_k,
        text_v,
        out_weight,
        hidden,
        text_len,
        head_mask,
        step_index,
        out_bias[None],
        final_shift,
        final_scale,
        final_weight,
        latent,
    )


def solution(mesh):
    in_specs = (
        P("cfg", ("seq", "head"), None),
        P("cfg", ("seq", "head"), None),
        P("cfg", ("seq", "head"), None),
        P("cfg", None, None),
        P("cfg", None, None),
        P("cfg"),
        P(),
        P("cfg", ("seq", "head"), None),
        P("head", None),
        P(),
        P("cfg", None),
        P("cfg", None),
        P(),
        P("cfg", ("seq", "head")),
        P(),
    )
    out_specs = (P("cfg", ("seq", "head")), P("cfg", ("seq", "head")))
    return jax.shard_map(shards, mesh=mesh, in_specs=in_specs, out_specs=out_specs, check_vma=False)
```

```python
import functools

import jax
import jax.numpy as jnp
from jax import lax
from jax.experimental import pallas as pl
from jax.experimental.pallas import tpu as pltpu
from jax.sharding import PartitionSpec as P

HDIM = 64
STEPS = 28
GUIDANCE = 3.5
GROUP_HEADS = 5
FEATURES = 320
TOKENS = 128
SLOTS = 384
QUERIES = 1024
TILE = 256
SCORE_SCALE = 0.125 * 1.4426950408889634
MESH = pl.DeviceIdType.MESH
f32 = jnp.float32
bf16 = jnp.bfloat16


def sigma_at(position):
    level = 1.0 - position.astype(jnp.float32) / STEPS
    return 3.0 * level / (1.0 + 2.0 * level)


def block_kernel(
    q_hbm,
    k_hbm,
    v_hbm,
    tk_hbm,
    tv_hbm,
    w_hbm,
    hidden_hbm,
    len_hbm,
    mask_hbm,
    bias_hbm,
    shift_hbm,
    scale_hbm,
    final_hbm,
    guided_ref,
    loaded,
    text_slab,
    q_stage,
    kv_stage,
    o_stage,
    q_recv,
    o_recv,
    kv,
    weight,
    qx,
    text_keys,
    text_values,
    s0,
    s1,
    p0,
    p1,
    m_ref,
    acc,
    hidden,
    attended,
    residual,
    v_stage,
    v_recv,
    len_ref,
    mask_ref,
    out_bias,
    shift_ref,
    scale_ref,
    final_weight,
    load_sem,
    q_send,
    q_recv_sem,
    a_send,
    a_recv,
    b_send,
    b_recv,
    o_send,
    o_recv_sem,
    w_send,
    w_recv,
    v_sem,
):
    cfg = lax.axis_index("cfg")
    seq = lax.axis_index("seq")
    group = lax.axis_index("head")
    core = lax.rem(seq, 2)
    parity = lax.rem(group, 2)
    row = group // 2
    right = lax.rem(seq + 2, 8)
    left = lax.rem(seq + 6, 8)
    sibling = seq + 1 - 2 * core
    far = lax.rem(seq + 2 + 4 * core, 8)
    turned = group + 1 - 2 * parity
    w_right = lax.rem(group + 2, 8)
    w_left = lax.rem(group + 6, 8)
    w_opposite = lax.rem(group + 4, 8)
    w_far = lax.rem(group + 2 + 4 * core, 8)

    slab_start = pl.multiple_of(128 * ((5 * group) // 2), 128)
    loads = (
        [
            pltpu.make_async_copy(src.at[0], loaded.at[i], load_sem.at[i])
            for i, src in enumerate((q_hbm, k_hbm, v_hbm))
        ]
        + [
            pltpu.make_async_copy(
                src.at[0, :, pl.ds(slab_start, 384)], text_slab.at[i], load_sem.at[3 + i]
            )
            for i, src in enumerate((tk_hbm, tv_hbm))
        ]
        + [
            pltpu.make_async_copy(
                w_hbm.at[pl.ds(160 * i, 160)], weight.at[2 * group + i], load_sem.at[5 + i]
            )
            for i in range(2)
        ]
        + [pltpu.make_async_copy(hidden_hbm.at[0], hidden, load_sem.at[7])]
        + [
            pltpu.make_async_copy(src, dst, load_sem.at[8 + i])
            for i, (src, dst) in enumerate(
                (
                    (bias_hbm, out_bias),
                    (shift_hbm, shift_ref),
                    (scale_hbm, scale_ref),
                    (final_hbm, final_weight),
                    (mask_hbm, mask_ref),
                    (len_hbm, len_ref),
                )
            )
        ]
    )
    for load in loads:
        load.start()

    barrier = pltpu.get_barrier_semaphore()
    for d in range(1, 8):
        pl.semaphore_signal(
            barrier, inc=1, device_id={"head": lax.rem(group + d, 8)}, device_id_type=MESH
        )
    for near in (right, left, sibling):
        pl.semaphore_signal(barrier, inc=1, device_id={"seq": near}, device_id_type=MESH)
    pl.semaphore_signal(barrier, inc=1, device_id={"cfg": 1 - cfg}, device_id_type=MESH)
    pl.semaphore_signal(
        barrier, inc=1, device_id={"cfg": 1 - cfg, "head": turned}, device_id_type=MESH
    )

    low = lax.broadcasted_iota(jnp.int32, (TOKENS, 128), 1) < HDIM
    low_half = lax.broadcasted_iota(jnp.int32, (HDIM, 128), 1) < HDIM

    loads[0].wait()
    for i in range(20):
        block = loaded[0, :, 128 * i : 128 * (i + 1)].T
        for half in range(2):
            f = 128 * i + HDIM * half
            q_stage[f // FEATURES, pl.ds(f % FEATURES, HDIM), :] = block[
                HDIM * half : HDIM * (half + 1)
            ]
    pl.semaphore_wait(barrier, 12)

    def head_copy(src, dst, send, recv, d):
        peer = lax.rem(group + d, 8)
        return pltpu.make_async_remote_copy(
            src_ref=src.at[peer],
            dst_ref=dst.at[0 if isinstance(d, int) else 1, row],
            send_sem=send.at[d],
            recv_sem=recv.at[d],
            device_id={"head": peer},
            device_id_type=MESH,
        )

    def q_copy(d):
        return head_copy(q_stage, q_recv, q_send, q_recv_sem, d)

    def kv_copy(d):
        return head_copy(kv_stage, kv, a_send, a_recv, d)

    along = (2, 6, 4)
    across = [lax.rem(1 + 2 * k + 6 * parity, 8) for k in range(4)]
    for d in along:
        q_copy(d).start()
    q_copy(across[0]).start()
    q_recv[0, pl.ds(row, 1)] = q_stage[pl.ds(group, 1)]

    loads[1].wait()
    loads[2].wait()
    for p in range(8):
        first = (5 * p) // 2
        tiles = [
            loaded[1, :, 128 * (first + i) : 128 * (first + i + 1)].astype(f32) for i in range(3)
        ]
        if p % 2 == 0:
            kv_stage[p, 0:128, :] = tiles[0].astype(bf16)
            kv_stage[p, 128:256, :] = tiles[1].astype(bf16)
            last = jnp.where(low_half, tiles[2][:HDIM], pltpu.roll(tiles[2][HDIM:], HDIM, 1))
        else:
            kv_stage[p, 0:128, :] = jnp.where(low, tiles[1], tiles[0]).astype(bf16)
            kv_stage[p, 128:256, :] = jnp.where(low, tiles[2], tiles[1]).astype(bf16)
            last = jnp.where(low_half, pltpu.roll(tiles[2][:HDIM], HDIM, 1), tiles[2][HDIM:])
        kv_stage[p, 256:320, :] = last.astype(bf16)
    for i in range(20):
        block = loaded[2, :, 128 * i : 128 * (i + 1)].T
        for half in range(2):
            f = 128 * i + HDIM * half
            kv_stage[f // FEATURES, pl.ds(FEATURES + f % FEATURES, HDIM), :] = block[
                HDIM * half : HDIM * (half + 1)
            ]
    for d in along:
        kv_copy(d).start()
    kv_copy(across[0]).start()
    kv[0, pl.ds(row, 1)] = kv_stage[pl.ds(group, 1)]

    loads[3].wait()
    loads[4].wait()
    odd = parity == 1
    swap = jnp.logical_and(lax.broadcasted_iota(jnp.int32, (SLOTS, 128), 1) < HDIM, odd)
    slabs = [text_slab[0, :, 128 * i : 128 * (i + 1)].astype(f32) for i in range(3)]
    text_keys[0] = jnp.where(swap, slabs[1], slabs[0]).astype(bf16)
    text_keys[1] = jnp.where(swap, slabs[2], slabs[1]).astype(bf16)
    text_keys[2] = slabs[2].astype(bf16)
    for i in range(3):
        for j in range(3):
            text_values[128 * i : 128 * (i + 1), 128 * j : 128 * (j + 1)] = text_slab[
                1, 128 * j : 128 * (j + 1), 128 * i : 128 * (i + 1)
            ].T

    zero = jnp.zeros((HDIM, TILE), bf16)
    ones = jnp.ones((16, 512), bf16)

    def queries_and_text(t, _):
        dead = lax.broadcasted_iota(jnp.int32, (SLOTS, TILE), 0) >= len_ref[0]
        for h in range(GROUP_HEADS):
            rows = slice(HDIM * h, HDIM * (h + 1))
            q = jnp.concatenate(
                [q_recv[t // 2, 2 * (t % 2), rows], q_recv[t // 2, 2 * (t % 2) + 1, rows]], 1
            )
            if h < 4:
                offset = parity if h % 2 == 0 else 1 - parity
                qx[6 * t + h, pl.ds(pl.multiple_of(HDIM * offset, HDIM), HDIM), :] = q
                qx[6 * t + h, pl.ds(pl.multiple_of(HDIM * (1 - offset), HDIM), HDIM), :] = zero
            else:
                for side in range(2):
                    qx[6 * t + 4 + side, HDIM * side : HDIM * (side + 1), :] = q
                    qx[6 * t + 4 + side, HDIM * (1 - side) : HDIM * (2 - side), :] = zero
        for h in range(GROUP_HEADS):
            weights_at = 6 * t + h if h < 4 else 6 * t + 4 + parity
            s = jnp.dot(text_keys[h // 2], qx[weights_at], preferred_element_type=f32)
            s = jnp.where(dead, -1e30, s)
            top = jnp.max(s, axis=0, keepdims=True)
            p = jnp.exp2((s - top) * SCORE_SCALE).astype(bf16)
            values = text_values[pl.ds(pl.multiple_of(HDIM * (parity + h), HDIM), HDIM), :]
            acc[GROUP_HEADS * t + h] = jnp.dot(
                jnp.concatenate([values, ones[:, :SLOTS]], 0), p, preferred_element_type=f32
            )
            m_ref[GROUP_HEADS * t + h] = top
        return 0

    loads[13].wait()
    for d in along:
        q_copy(d).wait_recv()
    for d in across[1:]:
        q_copy(d).start()
    lax.fori_loop(0, 2, queries_and_text, 0)

    def ring_copy(k, src, dst, target):
        return pltpu.make_async_remote_copy(
            src_ref=kv.at[src],
            dst_ref=kv.at[dst],
            send_sem=b_send.at[k],
            recv_sem=b_recv.at[dst],
            device_id={"seq": target},
            device_id_type=MESH,
        )

    copies = {
        0: (ring_copy(2, 0, 2, sibling), ring_copy(0, 0, 4, right), ring_copy(1, 0, 5, left)),
        1: (ring_copy(5, 1, 3, sibling), ring_copy(3, 1, 8, right), ring_copy(4, 1, 9, left)),
        2: (ring_copy(6, 4 + core, 12, far), ring_copy(7, 4, 6, sibling), ring_copy(8, 5, 7, sibling)),
        3: (ring_copy(9, 8 + core, 14, far), ring_copy(10, 8, 10, sibling), ring_copy(11, 9, 11, sibling)),
        4: (ring_copy(12, 12, 13, sibling),),
        5: (ring_copy(13, 14, 15, sibling),),
    }

    def arrived(*slots):
        for dst in slots:
            ring_copy(0, dst, dst, sibling).wait_recv()

    def send(stage):
        for copy in copies[stage]:
            copy.start()

    def weight_copy(k, owner, target, from_hbm=False):
        at = 2 * owner + core
        return pltpu.make_async_remote_copy(
            src_ref=w_hbm.at[pl.ds(pl.multiple_of(160 * core, 160), 160)] if from_hbm else weight.at[at],
            dst_ref=weight.at[at],
            send_sem=w_send.at[k],
            recv_sem=w_recv.at[k],
            device_id=target,
            device_id_type=MESH,
        )

    to_right, to_left = {"head": w_right}, {"head": w_left}
    to_turned = {"cfg": 1 - cfg, "head": turned}
    to_sibling = {"seq": sibling}
    owners = (
        w_left,
        w_right,
        turned,
        w_opposite,
        lax.rem(turned + 6, 8),
        lax.rem(turned + 2, 8),
        lax.rem(turned + 4, 8),
    )
    weight_copies = {
        0: (
            weight_copy(0, group, to_right, True),
            weight_copy(1, group, to_left, True),
            weight_copy(2, group, to_turned, True),
        ),
        1: (weight_copy(3, lax.rem(group + 6 + 4 * core, 8), {"head": w_far}),),
        2: (
            weight_copy(6, w_opposite, to_turned),
            weight_copy(4, turned, to_right),
            weight_copy(5, turned, to_left),
        ),
    }
    to_core = [weight_copy(7 + k, owners[k], to_sibling) for k in range(7)]

    def weight_arrived(*which):
        for k in which:
            weight_copy(k, group, to_sibling).wait_recv()

    def weight_send(stage):
        for copy in weight_copies[stage]:
            copy.start()

    def share(*which):
        for k in which:
            to_core[k].start()

    s_bufs = (s0, s1)
    p_bufs = (p0, p1)

    def score_parts(step, r, t, h, buf):
        for side in range(2):
            slot = step[side]
            if h < 4:
                for first in range(0, 4, 2):
                    lhs = jnp.concatenate(
                        [kv[slot, b, 128 * (h // 2) : 128 * (h // 2 + 1), :] for b in range(first, first + 2)], 0
                    )
                    s = jnp.dot(lhs, qx[6 * t + h], preferred_element_type=f32)
                    at = 512 * side + 128 * first
                    buf[at : at + 128 * 2, :] = s
                    yield jnp.max(s.reshape(16 * 2, 8, TILE), axis=0)
            else:
                lhs = jnp.concatenate([kv[slot, b, 256:320, :] for b in range(4)], 0)
                for half in range(2):
                    s = jnp.dot(lhs, qx[6 * t + 4 + half], preferred_element_type=f32)
                    for b in range(4):
                        at = 512 * side + 128 * b + HDIM * half
                        buf[at : at + HDIM, :] = s[HDIM * b : HDIM * (b + 1)]
                    yield jnp.max(s.reshape(32, 8, TILE), axis=0)

    def weigh_parts(buf, top, out):
        for j in range(0, QUERIES, 256):
            out[j : j + 256, :] = jnp.exp2((buf[j : j + 256, :] - top) * SCORE_SCALE).astype(bf16)
            yield None

    def value_parts(step, r, h, buf):
        for side in range(2):
            slot = step[side]
            rows = FEATURES + HDIM * h
            lhs = jnp.concatenate([kv[slot, b, rows : rows + HDIM, :] for b in range(4)], 1)
            yield jnp.dot(
                jnp.concatenate([lhs, ones], 0),
                buf[512 * side : 512 * (side + 1), :],
                preferred_element_type=f32,
            )

    def woven(*streams):
        given = [[] for _ in streams]
        waiting = [list_of for list_of in streams]
        live = list(range(len(streams)))
        while live:
            for i in tuple(live):
                try:
                    given[i].append(next(waiting[i]))
                except StopIteration:
                    live.remove(i)
        return given

    def new_top(r, parts):
        best = functools.reduce(jnp.maximum, parts)
        old = m_ref[r]
        new = jnp.maximum(old, jnp.max(best, axis=0, keepdims=True))
        m_ref[r] = new
        return new, jnp.exp2((old - new) * SCORE_SCALE)

    def finish(t, _):
        for h in range(GROUP_HEADS):
            sums = acc[GROUP_HEADS * t + h]
            gain = mask_ref[GROUP_HEADS * group + h].astype(f32)
            out = (sums[:HDIM] / sums[HDIM : HDIM + 1] * gain).astype(bf16)
            for side in range(2):
                o_stage[t // 2, 2 * (t % 2) + side, HDIM * h : HDIM * (h + 1), :] = out[
                    :, 128 * side : 128 * (side + 1)
                ]
        return 0

    def o_copy(d):
        peer = lax.rem(group + d, 8)
        return pltpu.make_async_remote_copy(
            src_ref=o_stage.at[0 if isinstance(d, int) else 1, peer // 2],
            dst_ref=o_recv.at[group],
            send_sem=o_send.at[d],
            recv_sem=o_recv_sem.at[d],
            device_id={"head": peer},
            device_id_type=MESH,
        )

    def at_start(half):
        @pl.when(half == 0)
        def _():
            for d in along:
                kv_copy(d).wait_recv()
            for d in across[1:]:
                kv_copy(d).start()
            send(0)
            arrived(2)

        @pl.when(half == 1)
        def _():
            for d in across:
                q_copy(d).wait_recv()
            lax.fori_loop(2, 4, queries_and_text, 0)

        @pl.when(half == 2)
        def _():
            for d in across:
                kv_copy(d).wait_recv()
            send(1)
            weight_send(0)
            arrived(3)

        @pl.when(half == 3)
        def _():
            arrived(4, 5)
            send(2)

        @pl.when(half == 6)
        def _():
            arrived(6, 7)

        @pl.when(half == 7)
        def _():
            arrived(12)
            send(4)
            weight_arrived(0, 1, 2)
            weight_send(1)
            share(0, 1, 2)

        @pl.when(half == 8)
        def _():
            arrived(13)

        @pl.when(half == 9)
        def _():
            arrived(8, 9)
            send(3)

        @pl.when(half == 10)
        def _():
            weight_arrived(3)
            weight_send(2)
            share(3)

        @pl.when(half == 12)
        def _():
            arrived(10, 11)

        @pl.when(half == 13)
        def _():
            arrived(14)
            send(5)

        @pl.when(half == 14)
        def _():
            arrived(15)

        @pl.when(half == 15)
        def _():
            loads[12].wait()
            lax.fori_loop(2, 4, finish, 0)
            for d in across:
                o_copy(d).start()
            weight_arrived(4, 5, 6)
            share(4, 5, 6)

    def half_step(half, _):
        at_start(half)
        order = half // 2
        slots = (
            jnp.where(order == 0, 0, jnp.where(order == 1, 1, 0)),
            jnp.where(order == 0, 2, jnp.where(order == 1, 3, 0)),
        )
        pair = jnp.where(
            order < 4, order, jnp.where(order == 4, 6, jnp.where(order < 7, order - 1, 7))
        )
        one = jnp.where(order < 2, slots[0], 2 * pair)
        two = jnp.where(order < 2, slots[1], 2 * pair + 1)
        side = jnp.where(order == 7, 1 - half % 2, half % 2)
        where = (one, two)

        def unit(j):
            return 10 * side + j, 2 * side + j // 5, j % 5

        (parts,) = woven(score_parts(where, *unit(0), s0))
        top, rescale = new_top(unit(0)[0], parts)
        before = None
        for j in range(10):
            streams = [weigh_parts(s_bufs[j % 2], top, p_bufs[j % 2])]
            if j < 9:
                streams.insert(0, score_parts(where, *unit(j + 1), s_bufs[(j + 1) % 2]))
            if j > 0:
                r, _, h = unit(j - 1)
                streams.append(value_parts(where, r, h, p_bufs[(j + 1) % 2]))
            given = woven(*streams)
            if j > 0:
                acc[r] = acc[r] * before + functools.reduce(jnp.add, given[-1])
            before = rescale
            if j < 9:
                top, rescale = new_top(unit(j + 1)[0], given[0])
        r, _, h = unit(9)
        (given,) = woven(value_parts(where, r, h, p1))
        acc[r] = acc[r] * before + functools.reduce(jnp.add, given)
        return 0

    lax.fori_loop(0, 16, half_step, 0)

    lax.fori_loop(0, 2, finish, 0)
    for d in along:
        o_copy(d).start()
    o_recv[pl.ds(group, 1)] = o_stage[0, pl.ds(row, 1)]

    for d in (*along, *across):
        q_copy(d).wait_send()
        kv_copy(d).wait_send()
    for stage in copies.values():
        for copy in stage:
            copy.wait_send()
    for stage in weight_copies.values():
        for copy in stage:
            copy.wait_send()

    for d in (*across, *along):
        o_copy(d).wait_recv()
    for p in range(8):
        for h in range(GROUP_HEADS):
            f = FEATURES * p + HDIM * h
            if f % 128 == 0:
                q = f // 128
                lo = o_recv[p, HDIM * h : HDIM * (h + 1), :]
                nxt = f + HDIM
                hi = o_recv[nxt // FEATURES, nxt % FEATURES : nxt % FEATURES + HDIM, :]
                attended[:, 128 * q : 128 * (q + 1)] = jnp.concatenate([lo, hi], 0).T
    for load in loads[5:12]:
        load.wait()
    weight_arrived(7, 8, 9, 10, 11, 12, 13)
    rows = attended[...]
    width = 2432
    total = None
    for n in range(0, width, TILE):
        cols = slice(n, min(n + TILE, width))
        part = jnp.dot(
            rows,
            jnp.concatenate([weight[i, :, cols] for i in range(16)], 0),
            preferred_element_type=f32,
        )
        part = hidden[:, cols].astype(f32) + part + out_bias[cols].astype(f32).reshape(1, -1)
        residual[:, cols] = part
        part = jnp.sum(part, axis=1, keepdims=True)
        total = part if total is None else total + part
    centre = total / width
    total = None
    for n in range(0, width, TILE):
        cols = slice(n, min(n + TILE, width))
        part = residual[:, cols] - centre
        residual[:, cols] = part
        part = jnp.sum(part * part, axis=1, keepdims=True)
        total = part if total is None else total + part
    norm = 1.0 / jnp.sqrt(total / width + 1e-06)
    velocity = None
    for n in range(0, width, TILE):
        cols = slice(n, min(n + TILE, width))
        modulated = residual[:, cols] * norm * (1.0 + scale_ref[:, cols].astype(f32)) + shift_ref[
            :, cols
        ].astype(f32)
        part = lax.dot_general(
            final_weight[:, cols],
            modulated.astype(bf16),
            (((1,), (1,)), ((), ())),
            preferred_element_type=f32,
        )
        velocity = part if velocity is None else velocity + part
    v_stage[0] = velocity[:32].astype(bf16)
    v_stage[1] = velocity[32:].astype(bf16)
    exchange = pltpu.make_async_remote_copy(
        src_ref=v_stage.at[1 - cfg],
        dst_ref=v_recv,
        send_sem=v_sem.at[0],
        recv_sem=v_sem.at[1],
        device_id={"cfg": 1 - cfg},
        device_id_type=MESH,
    )
    exchange.start()
    mine = jnp.where(cfg == 0, velocity[:32], velocity[32:])
    for d in (*along, *across):
        o_copy(d).wait_send()
    for copy in to_core:
        copy.wait_send()
    exchange.wait()
    theirs = v_recv[...].astype(f32)
    cond = jnp.where(cfg == 0, mine, theirs)
    uncond = jnp.where(cfg == 0, theirs, mine)
    guided_ref[...] = uncond + GUIDANCE * (cond - uncond)


def shards(
    q_img,
    k_img,
    v_img,
    text_k,
    text_v,
    text_len,
    head_mask,
    hidden,
    out_weight,
    out_bias,
    final_shift,
    final_scale,
    final_weight,
    latent,
    step_index,
):
    vmem = pltpu.VMEM
    dma = pltpu.SemaphoreType.DMA
    anywhere = pl.BlockSpec(memory_space=pl.ANY)
    whole = pl.BlockSpec(memory_space=pltpu.VMEM)
    guided = pl.pallas_call(
        block_kernel,
        out_shape=jax.ShapeDtypeStruct(latent.shape, f32),
        in_specs=[anywhere] * 13,
        out_specs=whole,
        scratch_shapes=[
            vmem((3, TOKENS, 2560), bf16),
            vmem((2, SLOTS, 384), bf16),
            vmem((8, FEATURES, TOKENS), bf16),
            vmem((8, 2 * FEATURES, TOKENS), bf16),
            vmem((2, 4, FEATURES, TOKENS), bf16),
            vmem((2, 4, FEATURES, TOKENS), bf16),
            vmem((8, FEATURES, TOKENS), bf16),
            vmem((16, 4, 2 * FEATURES, TOKENS), bf16),
            vmem((16, 160, 2432), bf16),
            vmem((24, 128, TILE), bf16),
            vmem((3, SLOTS, 128), bf16),
            vmem((384, SLOTS), bf16),
            vmem((QUERIES, TILE), f32),
            vmem((QUERIES, TILE), f32),
            vmem((QUERIES, TILE), bf16),
            vmem((QUERIES, TILE), bf16),
            vmem((20, 1, TILE), f32),
            vmem((20, 80, TILE), f32),
            vmem((TOKENS, 2432), bf16),
            vmem((TOKENS, 2560), bf16),
            vmem((TOKENS, 2432), f32),
            vmem((2, 32, TOKENS), bf16),
            vmem((32, TOKENS), bf16),
            pltpu.SMEM((1,), jnp.int32),
            pltpu.SMEM((40,), jnp.int32),
            vmem((2432,), bf16),
            vmem((1, 2432), bf16),
            vmem((1, 2432), bf16),
            vmem((64, 2432), bf16),
            dma((14,)),
            dma((8,)),
            dma((8,)),
            dma((8,)),
            dma((8,)),
            dma((14,)),
            dma((16,)),
            dma((8,)),
            dma((8,)),
            dma((14,)),
            dma((14,)),
            dma((2,)),
        ],
        compiler_params=pltpu.CompilerParams(
            collective_id=0, has_side_effects=True, vmem_limit_bytes=60 << 20
        ),
        cost_estimate=pl.CostEstimate(
            flops=40_000_000_000, bytes_accessed=20_000_000, transcendentals=44_000_000
        ),
    )(
        q_img,
        k_img,
        v_img,
        text_k,
        text_v,
        out_weight,
        hidden,
        text_len,
        head_mask,
        out_bias,
        final_shift,
        final_scale,
        final_weight,
    )
    sigma_now = sigma_at(step_index[0])
    sigma_next = sigma_at(step_index[0] + 1)
    denoised = latent - sigma_now * guided
    next_latent = latent + (sigma_next - sigma_now) * guided
    return (next_latent, denoised)


def solution(mesh):
    in_specs = (
        P("cfg", ("seq", "head"), None),
        P("cfg", ("seq", "head"), None),
        P("cfg", ("seq", "head"), None),
        P("cfg", None, None),
        P("cfg", None, None),
        P("cfg"),
        P(),
        P("cfg", ("seq", "head"), None),
        P("head", None),
        P(),
        P("cfg", None),
        P("cfg", None),
        P(),
        P("cfg", ("seq", "head")),
        P(),
    )
    out_specs = (P("cfg", ("seq", "head")), P("cfg", ("seq", "head")))
    return jax.shard_map(shards, mesh=mesh, in_specs=in_specs, out_specs=out_specs, check_vma=False)
```

```python
import functools

import jax
import jax.numpy as jnp
from jax import lax
from jax.experimental import pallas as pl
from jax.experimental.pallas import tpu as pltpu
from jax.sharding import PartitionSpec as P

HDIM = 64
STEPS = 28
GUIDANCE = 3.5
GROUP_HEADS = 5
FEATURES = 320
TOKENS = 128
SLOTS = 384
QUERIES = 1024
TILE = 256
SCORE_SCALE = 0.125 * 1.4426950408889634
MESH = pl.DeviceIdType.MESH
f32 = jnp.float32
bf16 = jnp.bfloat16


def sigma_at(position):
    level = 1.0 - position.astype(jnp.float32) / STEPS
    return 3.0 * level / (1.0 + 2.0 * level)


def block_kernel(
    q_hbm,
    k_hbm,
    v_hbm,
    tk_hbm,
    tv_hbm,
    w_hbm,
    hidden_hbm,
    len_hbm,
    mask_hbm,
    bias_hbm,
    shift_hbm,
    scale_hbm,
    final_hbm,
    guided_ref,
    loaded,
    text_slab,
    q_stage,
    kv_stage,
    o_stage,
    q_recv,
    o_recv,
    kv,
    weight,
    qx,
    text_keys,
    text_values,
    s0,
    s1,
    p0,
    p1,
    m_ref,
    acc,
    hidden,
    attended,
    residual,
    v_stage,
    v_recv,
    len_ref,
    mask_ref,
    out_bias,
    shift_ref,
    scale_ref,
    final_weight,
    load_sem,
    q_send,
    q_recv_sem,
    a_send,
    a_recv,
    b_send,
    b_recv,
    c_send,
    c_recv,
    o_send,
    o_recv_sem,
    w_send,
    w_recv,
    v_sem,
):
    cfg = lax.axis_index("cfg")
    seq = lax.axis_index("seq")
    group = lax.axis_index("head")
    core = lax.rem(seq, 2)
    parity = lax.rem(group, 2)
    row = group // 2
    right = lax.rem(seq + 2, 8)
    left = lax.rem(seq + 6, 8)
    sibling = seq + 1 - 2 * core
    far = lax.rem(seq + 2 + 4 * core, 8)
    turned = group + 1 - 2 * parity
    w_right = lax.rem(group + 2, 8)
    w_left = lax.rem(group + 6, 8)
    w_opposite = lax.rem(group + 4, 8)
    w_far = lax.rem(group + 2 + 4 * core, 8)

    slab_start = pl.multiple_of(128 * ((5 * group) // 2), 128)
    loads = (
        [
            pltpu.make_async_copy(src.at[0], loaded.at[i], load_sem.at[i])
            for i, src in enumerate((q_hbm, k_hbm, v_hbm))
        ]
        + [
            pltpu.make_async_copy(
                src.at[0, :, pl.ds(slab_start, 384)], text_slab.at[i], load_sem.at[3 + i]
            )
            for i, src in enumerate((tk_hbm, tv_hbm))
        ]
        + [
            pltpu.make_async_copy(
                w_hbm.at[pl.ds(160 * i, 160)], weight.at[2 * group + i], load_sem.at[5 + i]
            )
            for i in range(2)
        ]
        + [pltpu.make_async_copy(hidden_hbm.at[0], hidden, load_sem.at[7])]
        + [
            pltpu.make_async_copy(src, dst, load_sem.at[8 + i])
            for i, (src, dst) in enumerate(
                (
                    (bias_hbm, out_bias),
                    (shift_hbm, shift_ref),
                    (scale_hbm, scale_ref),
                    (final_hbm, final_weight),
                    (mask_hbm, mask_ref),
                    (len_hbm, len_ref),
                )
            )
        ]
    )
    for load in loads:
        load.start()

    barrier = pltpu.get_barrier_semaphore()
    for d in range(1, 8):
        pl.semaphore_signal(
            barrier, inc=1, device_id={"head": lax.rem(group + d, 8)}, device_id_type=MESH
        )
    for near in (right, left, sibling):
        pl.semaphore_signal(barrier, inc=1, device_id={"seq": near}, device_id_type=MESH)
    pl.semaphore_signal(barrier, inc=1, device_id={"cfg": 1 - cfg}, device_id_type=MESH)
    pl.semaphore_signal(
        barrier, inc=1, device_id={"cfg": 1 - cfg, "head": turned}, device_id_type=MESH
    )

    low = lax.broadcasted_iota(jnp.int32, (TOKENS, 128), 1) < HDIM
    low_half = lax.broadcasted_iota(jnp.int32, (HDIM, 128), 1) < HDIM

    loads[0].wait()
    for i in range(20):
        block = loaded[0, :, 128 * i : 128 * (i + 1)].T
        for half in range(2):
            f = 128 * i + HDIM * half
            q_stage[f // FEATURES, pl.ds(f % FEATURES, HDIM), :] = block[
                HDIM * half : HDIM * (half + 1)
            ]
    pl.semaphore_wait(barrier, 12)

    def head_copy(src, dst, send, recv, d):
        peer = lax.rem(group + d, 8)
        return pltpu.make_async_remote_copy(
            src_ref=src.at[peer],
            dst_ref=dst.at[0 if isinstance(d, int) else 1, row],
            send_sem=send.at[d],
            recv_sem=recv.at[d],
            device_id={"head": peer},
            device_id_type=MESH,
        )

    def q_copy(d):
        return head_copy(q_stage, q_recv, q_send, q_recv_sem, d)

    def kv_copy(d):
        return head_copy(kv_stage, kv, a_send, a_recv, d)

    along = (2, 6, 4)
    across = [lax.rem(1 + 2 * k + 6 * parity, 8) for k in range(4)]
    for d in along:
        q_copy(d).start()
    q_copy(across[0]).start()
    q_recv[0, pl.ds(row, 1)] = q_stage[pl.ds(group, 1)]

    loads[1].wait()
    loads[2].wait()
    for p in range(8):
        first = (5 * p) // 2
        tiles = [
            loaded[1, :, 128 * (first + i) : 128 * (first + i + 1)].astype(f32) for i in range(3)
        ]
        if p % 2 == 0:
            kv_stage[p, 0:128, :] = tiles[0].astype(bf16)
            kv_stage[p, 128:256, :] = tiles[1].astype(bf16)
            last = jnp.where(low_half, tiles[2][:HDIM], pltpu.roll(tiles[2][HDIM:], HDIM, 1))
        else:
            kv_stage[p, 0:128, :] = jnp.where(low, tiles[1], tiles[0]).astype(bf16)
            kv_stage[p, 128:256, :] = jnp.where(low, tiles[2], tiles[1]).astype(bf16)
            last = jnp.where(low_half, pltpu.roll(tiles[2][:HDIM], HDIM, 1), tiles[2][HDIM:])
        kv_stage[p, 256:320, :] = last.astype(bf16)
    for i in range(20):
        block = loaded[2, :, 128 * i : 128 * (i + 1)].T
        for half in range(2):
            f = 128 * i + HDIM * half
            kv_stage[f // FEATURES, pl.ds(FEATURES + f % FEATURES, HDIM), :] = block[
                HDIM * half : HDIM * (half + 1)
            ]
    for d in along:
        kv_copy(d).start()
    kv_copy(across[0]).start()
    kv[0, pl.ds(row, 1)] = kv_stage[pl.ds(group, 1)]

    def block_copy(k, d):
        at = lax.rem(group + 8 - d, 8) // 2
        return pltpu.make_async_remote_copy(
            src_ref=kv.at[k // 4, at],
            dst_ref=kv.at[2 + k // 4, at],
            send_sem=c_send.at[k],
            recv_sem=c_recv.at[k],
            device_id={"seq": sibling},
            device_id_type=MESH,
        )

    blocks = [block_copy(k, d) for k, d in enumerate((0, *along, *across))]
    blocks[0].start()

    loads[3].wait()
    loads[4].wait()
    odd = parity == 1
    swap = jnp.logical_and(lax.broadcasted_iota(jnp.int32, (SLOTS, 128), 1) < HDIM, odd)
    slabs = [text_slab[0, :, 128 * i : 128 * (i + 1)].astype(f32) for i in range(3)]
    text_keys[0] = jnp.where(swap, slabs[1], slabs[0]).astype(bf16)
    text_keys[1] = jnp.where(swap, slabs[2], slabs[1]).astype(bf16)
    text_keys[2] = slabs[2].astype(bf16)
    for i in range(3):
        for j in range(3):
            text_values[128 * i : 128 * (i + 1), 128 * j : 128 * (j + 1)] = text_slab[
                1, 128 * j : 128 * (j + 1), 128 * i : 128 * (i + 1)
            ].T

    zero = jnp.zeros((HDIM, TILE), bf16)
    ones = jnp.ones((16, 512), bf16)

    def queries_and_text(t, _):
        dead = lax.broadcasted_iota(jnp.int32, (SLOTS, TILE), 0) >= len_ref[0]
        for h in range(GROUP_HEADS):
            rows = slice(HDIM * h, HDIM * (h + 1))
            q = jnp.concatenate(
                [q_recv[t // 2, 2 * (t % 2), rows], q_recv[t // 2, 2 * (t % 2) + 1, rows]], 1
            )
            if h < 4:
                offset = parity if h % 2 == 0 else 1 - parity
                qx[6 * t + h, pl.ds(pl.multiple_of(HDIM * offset, HDIM), HDIM), :] = q
                qx[6 * t + h, pl.ds(pl.multiple_of(HDIM * (1 - offset), HDIM), HDIM), :] = zero
            else:
                for side in range(2):
                    qx[6 * t + 4 + side, HDIM * side : HDIM * (side + 1), :] = q
                    qx[6 * t + 4 + side, HDIM * (1 - side) : HDIM * (2 - side), :] = zero
        for h in range(GROUP_HEADS):
            weights_at = 6 * t + h if h < 4 else 6 * t + 4 + parity
            s = jnp.dot(text_keys[h // 2], qx[weights_at], preferred_element_type=f32)
            s = jnp.where(dead, -1e30, s)
            top = jnp.max(s, axis=0, keepdims=True)
            p = jnp.exp2((s - top) * SCORE_SCALE).astype(bf16)
            values = text_values[pl.ds(pl.multiple_of(HDIM * (parity + h), HDIM), HDIM), :]
            acc[GROUP_HEADS * t + h] = jnp.dot(
                jnp.concatenate([values, ones[:, :SLOTS]], 0), p, preferred_element_type=f32
            )
            m_ref[GROUP_HEADS * t + h] = top
        return 0

    loads[13].wait()
    for d in along:
        q_copy(d).wait_recv()
    for d in across[1:]:
        q_copy(d).start()
    lax.fori_loop(0, 2, queries_and_text, 0)

    def ring_copy(k, src, dst, target):
        return pltpu.make_async_remote_copy(
            src_ref=kv.at[src],
            dst_ref=kv.at[dst],
            send_sem=b_send.at[k],
            recv_sem=b_recv.at[dst],
            device_id={"seq": target},
            device_id_type=MESH,
        )

    copies = {
        0: (ring_copy(0, 0, 4, right), ring_copy(1, 0, 5, left)),
        1: (ring_copy(2, 1, 8, right), ring_copy(3, 1, 9, left)),
        2: (ring_copy(4, 4, 6, sibling), ring_copy(5, 5, 7, sibling)),
        3: (ring_copy(6, 4 + core, 12, far),),
        4: (ring_copy(7, 8 + core, 14, far), ring_copy(8, 8, 10, sibling), ring_copy(9, 9, 11, sibling)),
        5: (ring_copy(10, 12, 13, sibling), ring_copy(11, 14, 15, sibling)),
    }

    def arrived(*slots):
        for dst in slots:
            ring_copy(0, dst, dst, sibling).wait_recv()

    def send(stage):
        for copy in copies[stage]:
            copy.start()

    def weight_copy(k, owner, target, from_hbm=False):
        at = 2 * owner + core
        return pltpu.make_async_remote_copy(
            src_ref=w_hbm.at[pl.ds(pl.multiple_of(160 * core, 160), 160)] if from_hbm else weight.at[at],
            dst_ref=weight.at[at],
            send_sem=w_send.at[k],
            recv_sem=w_recv.at[k],
            device_id=target,
            device_id_type=MESH,
        )

    to_right, to_left = {"head": w_right}, {"head": w_left}
    to_turned = {"cfg": 1 - cfg, "head": turned}
    to_sibling = {"seq": sibling}
    owners = (
        w_left,
        w_right,
        turned,
        w_opposite,
        lax.rem(turned + 6, 8),
        lax.rem(turned + 2, 8),
        lax.rem(turned + 4, 8),
    )
    weight_copies = {
        0: (
            weight_copy(0, group, to_right, True),
            weight_copy(1, group, to_left, True),
            weight_copy(2, group, to_turned, True),
        ),
        1: (weight_copy(3, lax.rem(group + 6 + 4 * core, 8), {"head": w_far}),),
        2: (
            weight_copy(6, w_opposite, to_turned),
            weight_copy(4, turned, to_right),
            weight_copy(5, turned, to_left),
        ),
    }
    to_core = [weight_copy(7 + k, owners[k], to_sibling) for k in range(7)]

    def weight_arrived(*which):
        for k in which:
            weight_copy(k, group, to_sibling).wait_recv()

    def weight_send(stage):
        for copy in weight_copies[stage]:
            copy.start()

    def share(*which):
        for k in which:
            to_core[k].start()

    s_bufs = (s0, s1)
    p_bufs = (p0, p1)

    def score_parts(step, r, t, h, buf):
        for side in range(2):
            slot = step[side]
            if h < 4:
                for first in range(0, 4, 2):
                    lhs = jnp.concatenate(
                        [kv[slot, b, 128 * (h // 2) : 128 * (h // 2 + 1), :] for b in range(first, first + 2)], 0
                    )
                    s = jnp.dot(lhs, qx[6 * t + h], preferred_element_type=f32)
                    at = 512 * side + 128 * first
                    buf[at : at + 128 * 2, :] = s
                    yield jnp.max(s.reshape(16 * 2, 8, TILE), axis=0)
            else:
                lhs = jnp.concatenate([kv[slot, b, 256:320, :] for b in range(4)], 0)
                for half in range(2):
                    s = jnp.dot(lhs, qx[6 * t + 4 + half], preferred_element_type=f32)
                    for b in range(4):
                        at = 512 * side + 128 * b + HDIM * half
                        buf[at : at + HDIM, :] = s[HDIM * b : HDIM * (b + 1)]
                    yield jnp.max(s.reshape(32, 8, TILE), axis=0)

    def weigh_parts(buf, top, out):
        for j in range(0, QUERIES, 256):
            out[j : j + 256, :] = jnp.exp2((buf[j : j + 256, :] - top) * SCORE_SCALE).astype(bf16)
            yield None

    def value_parts(step, r, h, buf):
        for side in range(2):
            slot = step[side]
            rows = FEATURES + HDIM * h
            lhs = jnp.concatenate([kv[slot, b, rows : rows + HDIM, :] for b in range(4)], 1)
            yield jnp.dot(
                jnp.concatenate([lhs, ones], 0),
                buf[512 * side : 512 * (side + 1), :],
                preferred_element_type=f32,
            )

    def woven(*streams):
        given = [[] for _ in streams]
        waiting = [list_of for list_of in streams]
        live = list(range(len(streams)))
        while live:
            for i in tuple(live):
                try:
                    given[i].append(next(waiting[i]))
                except StopIteration:
                    live.remove(i)
        return given

    def new_top(r, parts):
        best = functools.reduce(jnp.maximum, parts)
        old = m_ref[r]
        new = jnp.maximum(old, jnp.max(best, axis=0, keepdims=True))
        m_ref[r] = new
        return new, jnp.exp2((old - new) * SCORE_SCALE)

    def finish(t, _):
        for h in range(GROUP_HEADS):
            sums = acc[GROUP_HEADS * t + h]
            gain = mask_ref[GROUP_HEADS * group + h].astype(f32)
            out = (sums[:HDIM] / sums[HDIM : HDIM + 1] * gain).astype(bf16)
            for side in range(2):
                o_stage[t // 2, 2 * (t % 2) + side, HDIM * h : HDIM * (h + 1), :] = out[
                    :, 128 * side : 128 * (side + 1)
                ]
        return 0

    def o_copy(d):
        peer = lax.rem(group + d, 8)
        return pltpu.make_async_remote_copy(
            src_ref=o_stage.at[0 if isinstance(d, int) else 1, peer // 2],
            dst_ref=o_recv.at[group],
            send_sem=o_send.at[d],
            recv_sem=o_recv_sem.at[d],
            device_id={"head": peer},
            device_id_type=MESH,
        )

    def at_start(half):
        @pl.when(half == 0)
        def _():
            for k, d in enumerate(along):
                kv_copy(d).wait_recv()
                blocks[1 + k].start()
            send(0)
            for d in across[1:]:
                kv_copy(d).start()
            for block in blocks[:4]:
                block.wait_recv()

        @pl.when(half == 1)
        def _():
            for d in across:
                q_copy(d).wait_recv()
            lax.fori_loop(2, 4, queries_and_text, 0)

        @pl.when(half == 2)
        def _():
            for k, d in enumerate(across):
                kv_copy(d).wait_recv()
                blocks[4 + k].start()
            send(1)
            weight_send(0)
            for block in blocks[4:]:
                block.wait_recv()

        @pl.when(half == 4)
        def _():
            arrived(4, 5)
            send(2)

        @pl.when(half == 6)
        def _():
            arrived(6, 7)
            send(3)

        @pl.when(half == 7)
        def _():
            weight_arrived(0, 1, 2)
            weight_send(1)
            share(0, 1, 2)

        @pl.when(half == 8)
        def _():
            arrived(8, 9)
            send(4)

        @pl.when(half == 10)
        def _():
            arrived(10, 11)
            weight_arrived(3)
            weight_send(2)
            share(3)

        @pl.when(half == 12)
        def _():
            arrived(12, 14)
            send(5)

        @pl.when(half == 14)
        def _():
            arrived(13, 15)

        @pl.when(half == 15)
        def _():
            loads[12].wait()
            lax.fori_loop(2, 4, finish, 0)
            for d in across:
                o_copy(d).start()

    def half_step(half, _):
        at_start(half)
        order = half // 2
        one = jnp.where(order < 2, order, jnp.where(order < 6, 2 * order, order + 6))
        two = jnp.where(order < 2, order + 2, jnp.where(order < 6, 2 * order + 1, order + 8))
        side = jnp.where(order == 7, 1 - half % 2, half % 2)
        where = (one, two)

        def unit(j):
            return 10 * side + j, 2 * side + j // 5, j % 5

        (parts,) = woven(score_parts(where, *unit(0), s0))
        top, rescale = new_top(unit(0)[0], parts)
        before = None
        for j in range(10):
            streams = [weigh_parts(s_bufs[j % 2], top, p_bufs[j % 2])]
            if j < 9:
                streams.insert(0, score_parts(where, *unit(j + 1), s_bufs[(j + 1) % 2]))
            if j > 0:
                r, _, h = unit(j - 1)
                streams.append(value_parts(where, r, h, p_bufs[(j + 1) % 2]))
            given = woven(*streams)
            if j > 0:
                acc[r] = acc[r] * before + functools.reduce(jnp.add, given[-1])
            before = rescale
            if j < 9:
                top, rescale = new_top(unit(j + 1)[0], given[0])
        r, _, h = unit(9)
        (given,) = woven(value_parts(where, r, h, p1))
        acc[r] = acc[r] * before + functools.reduce(jnp.add, given)
        return 0

    lax.fori_loop(0, 16, half_step, 0)

    lax.fori_loop(0, 2, finish, 0)
    for d in along:
        o_copy(d).start()
    weight_arrived(4, 5, 6)
    share(4, 5, 6)
    o_recv[pl.ds(group, 1)] = o_stage[0, pl.ds(row, 1)]

    for d in (*along, *across):
        q_copy(d).wait_send()
        kv_copy(d).wait_send()
    for block in blocks:
        block.wait_send()
    for stage in copies.values():
        for copy in stage:
            copy.wait_send()
    for stage in weight_copies.values():
        for copy in stage:
            copy.wait_send()

    for d in (*across, *along):
        o_copy(d).wait_recv()
    for p in range(8):
        for h in range(GROUP_HEADS):
            f = FEATURES * p + HDIM * h
            if f % 128 == 0:
                q = f // 128
                lo = o_recv[p, HDIM * h : HDIM * (h + 1), :]
                nxt = f + HDIM
                hi = o_recv[nxt // FEATURES, nxt % FEATURES : nxt % FEATURES + HDIM, :]
                attended[:, 128 * q : 128 * (q + 1)] = jnp.concatenate([lo, hi], 0).T
    for load in loads[5:12]:
        load.wait()
    weight_arrived(7, 8, 9, 10, 11, 12, 13)
    rows = attended[...]
    width = 2432
    total = None
    for n in range(0, width, TILE):
        cols = slice(n, min(n + TILE, width))
        part = jnp.dot(
            rows,
            jnp.concatenate([weight[i, :, cols] for i in range(16)], 0),
            preferred_element_type=f32,
        )
        part = hidden[:, cols].astype(f32) + part + out_bias[cols].astype(f32).reshape(1, -1)
        residual[:, cols] = part
        part = jnp.sum(part, axis=1, keepdims=True)
        total = part if total is None else total + part
    centre = total / width
    total = None
    for n in range(0, width, TILE):
        cols = slice(n, min(n + TILE, width))
        part = residual[:, cols] - centre
        residual[:, cols] = part
        part = jnp.sum(part * part, axis=1, keepdims=True)
        total = part if total is None else total + part
    norm = 1.0 / jnp.sqrt(total / width + 1e-06)
    velocity = None
    for n in range(0, width, TILE):
        cols = slice(n, min(n + TILE, width))
        modulated = residual[:, cols] * norm * (1.0 + scale_ref[:, cols].astype(f32)) + shift_ref[
            :, cols
        ].astype(f32)
        part = lax.dot_general(
            final_weight[:, cols],
            modulated.astype(bf16),
            (((1,), (1,)), ((), ())),
            preferred_element_type=f32,
        )
        velocity = part if velocity is None else velocity + part
    v_stage[0] = velocity[:32].astype(bf16)
    v_stage[1] = velocity[32:].astype(bf16)
    exchange = pltpu.make_async_remote_copy(
        src_ref=v_stage.at[1 - cfg],
        dst_ref=v_recv,
        send_sem=v_sem.at[0],
        recv_sem=v_sem.at[1],
        device_id={"cfg": 1 - cfg},
        device_id_type=MESH,
    )
    exchange.start()
    mine = jnp.where(cfg == 0, velocity[:32], velocity[32:])
    for d in (*along, *across):
        o_copy(d).wait_send()
    for copy in to_core:
        copy.wait_send()
    exchange.wait()
    theirs = v_recv[...].astype(f32)
    cond = jnp.where(cfg == 0, mine, theirs)
    uncond = jnp.where(cfg == 0, theirs, mine)
    guided_ref[...] = uncond + GUIDANCE * (cond - uncond)


def shards(
    q_img,
    k_img,
    v_img,
    text_k,
    text_v,
    text_len,
    head_mask,
    hidden,
    out_weight,
    out_bias,
    final_shift,
    final_scale,
    final_weight,
    latent,
    step_index,
):
    vmem = pltpu.VMEM
    dma = pltpu.SemaphoreType.DMA
    anywhere = pl.BlockSpec(memory_space=pl.ANY)
    whole = pl.BlockSpec(memory_space=pltpu.VMEM)
    guided = pl.pallas_call(
        block_kernel,
        out_shape=jax.ShapeDtypeStruct(latent.shape, f32),
        in_specs=[anywhere] * 13,
        out_specs=whole,
        scratch_shapes=[
            vmem((3, TOKENS, 2560), bf16),
            vmem((2, SLOTS, 384), bf16),
            vmem((8, FEATURES, TOKENS), bf16),
            vmem((8, 2 * FEATURES, TOKENS), bf16),
            vmem((2, 4, FEATURES, TOKENS), bf16),
            vmem((2, 4, FEATURES, TOKENS), bf16),
            vmem((8, FEATURES, TOKENS), bf16),
            vmem((16, 4, 2 * FEATURES, TOKENS), bf16),
            vmem((16, 160, 2432), bf16),
            vmem((24, 128, TILE), bf16),
            vmem((3, SLOTS, 128), bf16),
            vmem((384, SLOTS), bf16),
            vmem((QUERIES, TILE), f32),
            vmem((QUERIES, TILE), f32),
            vmem((QUERIES, TILE), bf16),
            vmem((QUERIES, TILE), bf16),
            vmem((20, 1, TILE), f32),
            vmem((20, 80, TILE), f32),
            vmem((TOKENS, 2432), bf16),
            vmem((TOKENS, 2560), bf16),
            vmem((TOKENS, 2432), f32),
            vmem((2, 32, TOKENS), bf16),
            vmem((32, TOKENS), bf16),
            pltpu.SMEM((1,), jnp.int32),
            pltpu.SMEM((40,), jnp.int32),
            vmem((2432,), bf16),
            vmem((1, 2432), bf16),
            vmem((1, 2432), bf16),
            vmem((64, 2432), bf16),
            dma((14,)),
            dma((8,)),
            dma((8,)),
            dma((8,)),
            dma((8,)),
            dma((12,)),
            dma((16,)),
            dma((8,)),
            dma((8,)),
            dma((8,)),
            dma((8,)),
            dma((14,)),
            dma((14,)),
            dma((2,)),
        ],
        compiler_params=pltpu.CompilerParams(
            collective_id=0, has_side_effects=True, vmem_limit_bytes=60 << 20
        ),
        cost_estimate=pl.CostEstimate(
            flops=40_000_000_000, bytes_accessed=20_000_000, transcendentals=44_000_000
        ),
    )(
        q_img,
        k_img,
        v_img,
        text_k,
        text_v,
        out_weight,
        hidden,
        text_len,
        head_mask,
        out_bias,
        final_shift,
        final_scale,
        final_weight,
    )
    sigma_now = sigma_at(step_index[0])
    sigma_next = sigma_at(step_index[0] + 1)
    denoised = latent - sigma_now * guided
    next_latent = latent + (sigma_next - sigma_now) * guided
    return (next_latent, denoised)


def solution(mesh):
    in_specs = (
        P("cfg", ("seq", "head"), None),
        P("cfg", ("seq", "head"), None),
        P("cfg", ("seq", "head"), None),
        P("cfg", None, None),
        P("cfg", None, None),
        P("cfg"),
        P(),
        P("cfg", ("seq", "head"), None),
        P("head", None),
        P(),
        P("cfg", None),
        P("cfg", None),
        P(),
        P("cfg", ("seq", "head")),
        P(),
    )
    out_specs = (P("cfg", ("seq", "head")), P("cfg", ("seq", "head")))
    return jax.shard_map(shards, mesh=mesh, in_specs=in_specs, out_specs=out_specs, check_vma=False)
```

```python
import functools

import jax
import jax.numpy as jnp
from jax import lax
from jax.experimental import pallas as pl
from jax.experimental.pallas import tpu as pltpu
from jax.sharding import PartitionSpec as P

HDIM = 64
STEPS = 28
GUIDANCE = 3.5
GROUP_HEADS = 5
FEATURES = 320
TOKENS = 128
SLOTS = 384
QUERIES = 1024
TILE = 256
SCORE_SCALE = 0.125 * 1.4426950408889634
MESH = pl.DeviceIdType.MESH
f32 = jnp.float32
bf16 = jnp.bfloat16


def sigma_at(position):
    level = 1.0 - position.astype(jnp.float32) / STEPS
    return 3.0 * level / (1.0 + 2.0 * level)


def block_kernel(
    q_hbm,
    k_hbm,
    v_hbm,
    tk_hbm,
    tv_hbm,
    w_hbm,
    hidden_hbm,
    len_hbm,
    mask_hbm,
    bias_hbm,
    shift_hbm,
    scale_hbm,
    final_hbm,
    guided_ref,
    loaded,
    text_slab,
    q_stage,
    kv_stage,
    o_stage,
    q_recv,
    o_recv,
    kv,
    weight,
    qx,
    text_keys,
    text_values,
    s0,
    s1,
    p0,
    p1,
    m_ref,
    acc,
    hidden,
    attended,
    residual,
    v_stage,
    v_recv,
    len_ref,
    mask_ref,
    out_bias,
    shift_ref,
    scale_ref,
    final_weight,
    load_sem,
    q_send,
    q_recv_sem,
    a_send,
    a_recv,
    b_send,
    b_recv,
    c_send,
    c_recv,
    o_send,
    o_recv_sem,
    w_send,
    w_recv,
    v_sem,
):
    cfg = lax.axis_index("cfg")
    seq = lax.axis_index("seq")
    group = lax.axis_index("head")
    core = lax.rem(seq, 2)
    parity = lax.rem(group, 2)
    row = group // 2
    right = lax.rem(seq + 2, 8)
    left = lax.rem(seq + 6, 8)
    sibling = seq + 1 - 2 * core
    far = lax.rem(seq + 2 + 4 * core, 8)
    turned = group + 1 - 2 * parity
    w_right = lax.rem(group + 2, 8)
    w_left = lax.rem(group + 6, 8)
    w_opposite = lax.rem(group + 4, 8)
    w_far = lax.rem(group + 2 + 4 * core, 8)

    slab_start = pl.multiple_of(128 * ((5 * group) // 2), 128)
    loads = (
        [
            pltpu.make_async_copy(src.at[0], loaded.at[i], load_sem.at[i])
            for i, src in enumerate((q_hbm, k_hbm, v_hbm))
        ]
        + [
            pltpu.make_async_copy(
                src.at[0, :, pl.ds(slab_start, 384)], text_slab.at[i], load_sem.at[3 + i]
            )
            for i, src in enumerate((tk_hbm, tv_hbm))
        ]
        + [
            pltpu.make_async_copy(
                w_hbm.at[pl.ds(160 * i, 160)], weight.at[2 * group + i], load_sem.at[5 + i]
            )
            for i in range(2)
        ]
        + [pltpu.make_async_copy(hidden_hbm.at[0], hidden, load_sem.at[7])]
        + [
            pltpu.make_async_copy(src, dst, load_sem.at[8 + i])
            for i, (src, dst) in enumerate(
                (
                    (bias_hbm, out_bias),
                    (shift_hbm, shift_ref),
                    (scale_hbm, scale_ref),
                    (final_hbm, final_weight),
                    (mask_hbm, mask_ref),
                    (len_hbm, len_ref),
                )
            )
        ]
    )
    for load in loads:
        load.start()

    barrier = pltpu.get_barrier_semaphore()
    for d in range(1, 8):
        pl.semaphore_signal(
            barrier, inc=1, device_id={"head": lax.rem(group + d, 8)}, device_id_type=MESH
        )
    for near in (right, left, sibling):
        pl.semaphore_signal(barrier, inc=1, device_id={"seq": near}, device_id_type=MESH)
    pl.semaphore_signal(barrier, inc=1, device_id={"cfg": 1 - cfg}, device_id_type=MESH)
    pl.semaphore_signal(
        barrier, inc=1, device_id={"cfg": 1 - cfg, "head": turned}, device_id_type=MESH
    )

    low = lax.broadcasted_iota(jnp.int32, (TOKENS, 128), 1) < HDIM
    low_half = lax.broadcasted_iota(jnp.int32, (HDIM, 128), 1) < HDIM

    loads[0].wait()
    for i in range(20):
        block = loaded[0, :, 128 * i : 128 * (i + 1)].T
        for half in range(2):
            f = 128 * i + HDIM * half
            q_stage[f // FEATURES, pl.ds(f % FEATURES, HDIM), :] = block[
                HDIM * half : HDIM * (half + 1)
            ]
    pl.semaphore_wait(barrier, 12)

    def head_copy(src, dst, send, recv, d):
        peer = lax.rem(group + d, 8)
        return pltpu.make_async_remote_copy(
            src_ref=src.at[peer],
            dst_ref=dst.at[0 if isinstance(d, int) else 1, row],
            send_sem=send.at[d],
            recv_sem=recv.at[d],
            device_id={"head": peer},
            device_id_type=MESH,
        )

    def q_copy(d):
        return head_copy(q_stage, q_recv, q_send, q_recv_sem, d)

    def kv_copy(d):
        return head_copy(kv_stage, kv, a_send, a_recv, d)

    along = (2, 6, 4)
    across = [lax.rem(1 + 2 * k + 6 * parity, 8) for k in range(4)]
    for d in along:
        q_copy(d).start()
    for d in across:
        q_copy(d).start()
    q_recv[0, pl.ds(row, 1)] = q_stage[pl.ds(group, 1)]

    loads[1].wait()
    loads[2].wait()
    for p in range(8):
        first = (5 * p) // 2
        tiles = [
            loaded[1, :, 128 * (first + i) : 128 * (first + i + 1)].astype(f32) for i in range(3)
        ]
        if p % 2 == 0:
            kv_stage[p, 0:128, :] = tiles[0].astype(bf16)
            kv_stage[p, 128:256, :] = tiles[1].astype(bf16)
            last = jnp.where(low_half, tiles[2][:HDIM], pltpu.roll(tiles[2][HDIM:], HDIM, 1))
        else:
            kv_stage[p, 0:128, :] = jnp.where(low, tiles[1], tiles[0]).astype(bf16)
            kv_stage[p, 128:256, :] = jnp.where(low, tiles[2], tiles[1]).astype(bf16)
            last = jnp.where(low_half, pltpu.roll(tiles[2][:HDIM], HDIM, 1), tiles[2][HDIM:])
        kv_stage[p, 256:320, :] = last.astype(bf16)
    for i in range(20):
        block = loaded[2, :, 128 * i : 128 * (i + 1)].T
        for half in range(2):
            f = 128 * i + HDIM * half
            kv_stage[f // FEATURES, pl.ds(FEATURES + f % FEATURES, HDIM), :] = block[
                HDIM * half : HDIM * (half + 1)
            ]
    for d in along:
        kv_copy(d).start()
    kv_copy(across[0]).start()
    kv[0, pl.ds(row, 1)] = kv_stage[pl.ds(group, 1)]

    def block_copy(k, d):
        at = lax.rem(group + 8 - d, 8) // 2
        return pltpu.make_async_remote_copy(
            src_ref=kv.at[k // 4, at],
            dst_ref=kv.at[2 + k // 4, at],
            send_sem=c_send.at[k],
            recv_sem=c_recv.at[k],
            device_id={"seq": sibling},
            device_id_type=MESH,
        )

    blocks = [block_copy(k, d) for k, d in enumerate((0, *along, *across))]
    blocks[0].start()

    loads[3].wait()
    loads[4].wait()
    odd = parity == 1
    swap = jnp.logical_and(lax.broadcasted_iota(jnp.int32, (SLOTS, 128), 1) < HDIM, odd)
    slabs = [text_slab[0, :, 128 * i : 128 * (i + 1)].astype(f32) for i in range(3)]
    text_keys[0] = jnp.where(swap, slabs[1], slabs[0]).astype(bf16)
    text_keys[1] = jnp.where(swap, slabs[2], slabs[1]).astype(bf16)
    text_keys[2] = slabs[2].astype(bf16)
    for i in range(3):
        for j in range(3):
            text_values[128 * i : 128 * (i + 1), 128 * j : 128 * (j + 1)] = text_slab[
                1, 128 * j : 128 * (j + 1), 128 * i : 128 * (i + 1)
            ].T

    zero = jnp.zeros((HDIM, TILE), bf16)
    ones = jnp.ones((16, 512), bf16)

    def queries_and_text(t, _):
        dead = lax.broadcasted_iota(jnp.int32, (SLOTS, TILE), 0) >= len_ref[0]
        for h in range(GROUP_HEADS):
            rows = slice(HDIM * h, HDIM * (h + 1))
            q = jnp.concatenate(
                [q_recv[t // 2, 2 * (t % 2), rows], q_recv[t // 2, 2 * (t % 2) + 1, rows]], 1
            )
            if h < 4:
                offset = parity if h % 2 == 0 else 1 - parity
                qx[6 * t + h, pl.ds(pl.multiple_of(HDIM * offset, HDIM), HDIM), :] = q
                qx[6 * t + h, pl.ds(pl.multiple_of(HDIM * (1 - offset), HDIM), HDIM), :] = zero
            else:
                for side in range(2):
                    qx[6 * t + 4 + side, HDIM * side : HDIM * (side + 1), :] = q
                    qx[6 * t + 4 + side, HDIM * (1 - side) : HDIM * (2 - side), :] = zero
        for h in range(GROUP_HEADS):
            weights_at = 6 * t + h if h < 4 else 6 * t + 4 + parity
            s = jnp.dot(text_keys[h // 2], qx[weights_at], preferred_element_type=f32)
            s = jnp.where(dead, -1e30, s)
            top = jnp.max(s, axis=0, keepdims=True)
            p = jnp.exp2((s - top) * SCORE_SCALE).astype(bf16)
            values = text_values[pl.ds(pl.multiple_of(HDIM * (parity + h), HDIM), HDIM), :]
            acc[GROUP_HEADS * t + h] = jnp.dot(
                jnp.concatenate([values, ones[:, :SLOTS]], 0), p, preferred_element_type=f32
            )
            m_ref[GROUP_HEADS * t + h] = top
        return 0

    loads[13].wait()
    for d in along:
        q_copy(d).wait_recv()
    lax.fori_loop(0, 2, queries_and_text, 0)

    def ring_copy(k, src, dst, target):
        return pltpu.make_async_remote_copy(
            src_ref=kv.at[src],
            dst_ref=kv.at[dst],
            send_sem=b_send.at[k],
            recv_sem=b_recv.at[dst],
            device_id={"seq": target},
            device_id_type=MESH,
        )

    copies = {
        0: (ring_copy(0, 0, 4, right), ring_copy(1, 0, 5, left)),
        1: (ring_copy(2, 1, 8, right), ring_copy(3, 1, 9, left)),
        2: (ring_copy(4, 4, 6, sibling), ring_copy(5, 5, 7, sibling)),
        3: (ring_copy(6, 4 + core, 12, far),),
        4: (ring_copy(7, 8 + core, 14, far), ring_copy(8, 8, 10, sibling), ring_copy(9, 9, 11, sibling)),
        5: (ring_copy(10, 12, 13, sibling), ring_copy(11, 14, 15, sibling)),
    }

    def arrived(*slots):
        for dst in slots:
            ring_copy(0, dst, dst, sibling).wait_recv()

    def send(stage):
        for copy in copies[stage]:
            copy.start()

    def weight_copy(k, owner, target, from_hbm=False):
        at = 2 * owner + core
        return pltpu.make_async_remote_copy(
            src_ref=w_hbm.at[pl.ds(pl.multiple_of(160 * core, 160), 160)] if from_hbm else weight.at[at],
            dst_ref=weight.at[at],
            send_sem=w_send.at[k],
            recv_sem=w_recv.at[k],
            device_id=target,
            device_id_type=MESH,
        )

    to_right, to_left = {"head": w_right}, {"head": w_left}
    to_turned = {"cfg": 1 - cfg, "head": turned}
    to_sibling = {"seq": sibling}
    owners = (
        w_left,
        w_right,
        turned,
        w_opposite,
        lax.rem(turned + 6, 8),
        lax.rem(turned + 2, 8),
        lax.rem(turned + 4, 8),
    )
    weight_copies = {
        0: (
            weight_copy(0, group, to_right, True),
            weight_copy(1, group, to_left, True),
            weight_copy(2, group, to_turned, True),
        ),
        1: (weight_copy(3, lax.rem(group + 6 + 4 * core, 8), {"head": w_far}),),
        2: (
            weight_copy(6, w_opposite, to_turned),
            weight_copy(4, turned, to_right),
            weight_copy(5, turned, to_left),
        ),
    }
    to_core = [weight_copy(7 + k, owners[k], to_sibling) for k in range(7)]

    def weight_arrived(*which):
        for k in which:
            weight_copy(k, group, to_sibling).wait_recv()

    def weight_send(stage):
        for copy in weight_copies[stage]:
            copy.start()

    def share(*which):
        for k in which:
            to_core[k].start()

    s_bufs = (s0, s1)
    p_bufs = (p0, p1)

    def score_parts(step, r, t, h, buf):
        for side in range(2):
            slot = step[side]
            if h < 4:
                for first in range(0, 4, 2):
                    lhs = jnp.concatenate(
                        [kv[slot, b, 128 * (h // 2) : 128 * (h // 2 + 1), :] for b in range(first, first + 2)], 0
                    )
                    s = jnp.dot(lhs, qx[6 * t + h], preferred_element_type=f32)
                    at = 512 * side + 128 * first
                    buf[at : at + 128 * 2, :] = s
                    yield jnp.max(s.reshape(16 * 2, 8, TILE), axis=0)
            else:
                lhs = jnp.concatenate([kv[slot, b, 256:320, :] for b in range(4)], 0)
                for half in range(2):
                    s = jnp.dot(lhs, qx[6 * t + 4 + half], preferred_element_type=f32)
                    for b in range(4):
                        at = 512 * side + 128 * b + HDIM * half
                        buf[at : at + HDIM, :] = s[HDIM * b : HDIM * (b + 1)]
                    yield jnp.max(s.reshape(32, 8, TILE), axis=0)

    def weigh_parts(buf, top, out):
        for j in range(0, QUERIES, 256):
            out[j : j + 256, :] = jnp.exp2((buf[j : j + 256, :] - top) * SCORE_SCALE).astype(bf16)
            yield None

    def value_parts(step, r, h, buf):
        for side in range(2):
            slot = step[side]
            rows = FEATURES + HDIM * h
            lhs = jnp.concatenate([kv[slot, b, rows : rows + HDIM, :] for b in range(4)], 1)
            yield jnp.dot(
                jnp.concatenate([lhs, ones], 0),
                buf[512 * side : 512 * (side + 1), :],
                preferred_element_type=f32,
            )

    def woven(*streams):
        given = [[] for _ in streams]
        waiting = [list_of for list_of in streams]
        live = list(range(len(streams)))
        while live:
            for i in tuple(live):
                try:
                    given[i].append(next(waiting[i]))
                except StopIteration:
                    live.remove(i)
        return given

    def new_top(r, parts):
        best = functools.reduce(jnp.maximum, parts)
        old = m_ref[r]
        new = jnp.maximum(old, jnp.max(best, axis=0, keepdims=True))
        m_ref[r] = new
        return new, jnp.exp2((old - new) * SCORE_SCALE)

    def finish(t, _):
        for h in range(GROUP_HEADS):
            sums = acc[GROUP_HEADS * t + h]
            gain = mask_ref[GROUP_HEADS * group + h].astype(f32)
            out = (sums[:HDIM] / sums[HDIM : HDIM + 1] * gain).astype(bf16)
            for side in range(2):
                o_stage[t // 2, 2 * (t % 2) + side, HDIM * h : HDIM * (h + 1), :] = out[
                    :, 128 * side : 128 * (side + 1)
                ]
        return 0

    def o_copy(d):
        peer = lax.rem(group + d, 8)
        return pltpu.make_async_remote_copy(
            src_ref=o_stage.at[0 if isinstance(d, int) else 1, peer // 2],
            dst_ref=o_recv.at[group],
            send_sem=o_send.at[d],
            recv_sem=o_recv_sem.at[d],
            device_id={"head": peer},
            device_id_type=MESH,
        )

    def at_start(half):
        @pl.when(half == 0)
        def _():
            for k, d in enumerate(along):
                kv_copy(d).wait_recv()
                blocks[1 + k].start()
            send(0)
            for d in across[1:]:
                kv_copy(d).start()
            for block in blocks[:4]:
                block.wait_recv()

        @pl.when(half == 1)
        def _():
            for d in across:
                q_copy(d).wait_recv()
            lax.fori_loop(2, 4, queries_and_text, 0)

        @pl.when(half == 2)
        def _():
            for k, d in enumerate(across):
                kv_copy(d).wait_recv()
                blocks[4 + k].start()
            send(1)
            weight_send(0)
            for block in blocks[4:]:
                block.wait_recv()

        @pl.when(half == 4)
        def _():
            arrived(4, 5)
            send(2)

        @pl.when(half == 6)
        def _():
            arrived(6, 7)
            send(3)

        @pl.when(half == 7)
        def _():
            weight_arrived(0, 1, 2)
            weight_send(1)
            share(0, 1, 2)

        @pl.when(half == 8)
        def _():
            arrived(8, 9)
            send(4)

        @pl.when(half == 10)
        def _():
            arrived(10, 11)
            weight_arrived(3)
            weight_send(2)
            share(3)

        @pl.when(half == 12)
        def _():
            arrived(12, 14)
            send(5)

        @pl.when(half == 14)
        def _():
            arrived(13, 15)

        @pl.when(half == 15)
        def _():
            loads[12].wait()
            lax.fori_loop(2, 4, finish, 0)
            for d in across:
                o_copy(d).start()

    def half_step(half, _):
        at_start(half)
        order = half // 2
        one = jnp.where(order < 2, order, jnp.where(order < 6, 2 * order, order + 6))
        two = jnp.where(order < 2, order + 2, jnp.where(order < 6, 2 * order + 1, order + 8))
        side = jnp.where(order == 7, 1 - half % 2, half % 2)
        where = (one, two)

        def unit(j):
            return 10 * side + j, 2 * side + j // 5, j % 5

        (parts,) = woven(score_parts(where, *unit(0), s0))
        top, rescale = new_top(unit(0)[0], parts)
        before = None
        for j in range(10):
            streams = [weigh_parts(s_bufs[j % 2], top, p_bufs[j % 2])]
            if j < 9:
                streams.insert(0, score_parts(where, *unit(j + 1), s_bufs[(j + 1) % 2]))
            if j > 0:
                r, _, h = unit(j - 1)
                streams.append(value_parts(where, r, h, p_bufs[(j + 1) % 2]))
            given = woven(*streams)
            if j > 0:
                acc[r] = acc[r] * before + functools.reduce(jnp.add, given[-1])
            before = rescale
            if j < 9:
                top, rescale = new_top(unit(j + 1)[0], given[0])
        r, _, h = unit(9)
        (given,) = woven(value_parts(where, r, h, p1))
        acc[r] = acc[r] * before + functools.reduce(jnp.add, given)
        return 0

    lax.fori_loop(0, 16, half_step, 0)

    lax.fori_loop(0, 2, finish, 0)
    for d in along:
        o_copy(d).start()
    weight_arrived(4, 5, 6)
    share(4, 5, 6)
    o_recv[pl.ds(group, 1)] = o_stage[0, pl.ds(row, 1)]

    for d in (*along, *across):
        q_copy(d).wait_send()
        kv_copy(d).wait_send()
    for block in blocks:
        block.wait_send()
    for stage in copies.values():
        for copy in stage:
            copy.wait_send()
    for stage in weight_copies.values():
        for copy in stage:
            copy.wait_send()

    for d in (*across, *along):
        o_copy(d).wait_recv()
    for p in range(8):
        for h in range(GROUP_HEADS):
            f = FEATURES * p + HDIM * h
            if f % 128 == 0:
                q = f // 128
                lo = o_recv[p, HDIM * h : HDIM * (h + 1), :]
                nxt = f + HDIM
                hi = o_recv[nxt // FEATURES, nxt % FEATURES : nxt % FEATURES + HDIM, :]
                attended[:, 128 * q : 128 * (q + 1)] = jnp.concatenate([lo, hi], 0).T
    for load in loads[5:12]:
        load.wait()
    weight_arrived(7, 8, 9, 10, 11, 12, 13)
    rows = attended[...]
    width = 2432
    total = None
    for n in range(0, width, TILE):
        cols = slice(n, min(n + TILE, width))
        part = jnp.dot(
            rows,
            jnp.concatenate([weight[i, :, cols] for i in range(16)], 0),
            preferred_element_type=f32,
        )
        part = hidden[:, cols].astype(f32) + part + out_bias[cols].astype(f32).reshape(1, -1)
        residual[:, cols] = part
        part = jnp.sum(part, axis=1, keepdims=True)
        total = part if total is None else total + part
    centre = total / width
    total = None
    for n in range(0, width, TILE):
        cols = slice(n, min(n + TILE, width))
        part = residual[:, cols] - centre
        residual[:, cols] = part
        part = jnp.sum(part * part, axis=1, keepdims=True)
        total = part if total is None else total + part
    norm = 1.0 / jnp.sqrt(total / width + 1e-06)
    velocity = None
    for n in range(0, width, TILE):
        cols = slice(n, min(n + TILE, width))
        modulated = residual[:, cols] * norm * (1.0 + scale_ref[:, cols].astype(f32)) + shift_ref[
            :, cols
        ].astype(f32)
        part = lax.dot_general(
            final_weight[:, cols],
            modulated.astype(bf16),
            (((1,), (1,)), ((), ())),
            preferred_element_type=f32,
        )
        velocity = part if velocity is None else velocity + part
    v_stage[0] = velocity[:32].astype(bf16)
    v_stage[1] = velocity[32:].astype(bf16)
    exchange = pltpu.make_async_remote_copy(
        src_ref=v_stage.at[1 - cfg],
        dst_ref=v_recv,
        send_sem=v_sem.at[0],
        recv_sem=v_sem.at[1],
        device_id={"cfg": 1 - cfg},
        device_id_type=MESH,
    )
    exchange.start()
    mine = jnp.where(cfg == 0, velocity[:32], velocity[32:])
    for d in (*along, *across):
        o_copy(d).wait_send()
    for copy in to_core:
        copy.wait_send()
    exchange.wait()
    theirs = v_recv[...].astype(f32)
    cond = jnp.where(cfg == 0, mine, theirs)
    uncond = jnp.where(cfg == 0, theirs, mine)
    guided_ref[...] = uncond + GUIDANCE * (cond - uncond)


def shards(
    q_img,
    k_img,
    v_img,
    text_k,
    text_v,
    text_len,
    head_mask,
    hidden,
    out_weight,
    out_bias,
    final_shift,
    final_scale,
    final_weight,
    latent,
    step_index,
):
    vmem = pltpu.VMEM
    dma = pltpu.SemaphoreType.DMA
    anywhere = pl.BlockSpec(memory_space=pl.ANY)
    whole = pl.BlockSpec(memory_space=pltpu.VMEM)
    guided = pl.pallas_call(
        block_kernel,
        out_shape=jax.ShapeDtypeStruct(latent.shape, f32),
        in_specs=[anywhere] * 13,
        out_specs=whole,
        scratch_shapes=[
            vmem((3, TOKENS, 2560), bf16),
            vmem((2, SLOTS, 384), bf16),
            vmem((8, FEATURES, TOKENS), bf16),
            vmem((8, 2 * FEATURES, TOKENS), bf16),
            vmem((2, 4, FEATURES, TOKENS), bf16),
            vmem((2, 4, FEATURES, TOKENS), bf16),
            vmem((8, FEATURES, TOKENS), bf16),
            vmem((16, 4, 2 * FEATURES, TOKENS), bf16),
            vmem((16, 160, 2432), bf16),
            vmem((24, 128, TILE), bf16),
            vmem((3, SLOTS, 128), bf16),
            vmem((384, SLOTS), bf16),
            vmem((QUERIES, TILE), f32),
            vmem((QUERIES, TILE), f32),
            vmem((QUERIES, TILE), bf16),
            vmem((QUERIES, TILE), bf16),
            vmem((20, 1, TILE), f32),
            vmem((20, 80, TILE), f32),
            vmem((TOKENS, 2432), bf16),
            vmem((TOKENS, 2560), bf16),
            vmem((TOKENS, 2432), f32),
            vmem((2, 32, TOKENS), bf16),
            vmem((32, TOKENS), bf16),
            pltpu.SMEM((1,), jnp.int32),
            pltpu.SMEM((40,), jnp.int32),
            vmem((2432,), bf16),
            vmem((1, 2432), bf16),
            vmem((1, 2432), bf16),
            vmem((64, 2432), bf16),
            dma((14,)),
            dma((8,)),
            dma((8,)),
            dma((8,)),
            dma((8,)),
            dma((12,)),
            dma((16,)),
            dma((8,)),
            dma((8,)),
            dma((8,)),
            dma((8,)),
            dma((14,)),
            dma((14,)),
            dma((2,)),
        ],
        compiler_params=pltpu.CompilerParams(
            collective_id=0, has_side_effects=True, vmem_limit_bytes=60 << 20
        ),
        cost_estimate=pl.CostEstimate(
            flops=40_000_000_000, bytes_accessed=20_000_000, transcendentals=44_000_000
        ),
    )(
        q_img,
        k_img,
        v_img,
        text_k,
        text_v,
        out_weight,
        hidden,
        text_len,
        head_mask,
        out_bias,
        final_shift,
        final_scale,
        final_weight,
    )
    sigma_now = sigma_at(step_index[0])
    sigma_next = sigma_at(step_index[0] + 1)
    denoised = latent - sigma_now * guided
    next_latent = latent + (sigma_next - sigma_now) * guided
    return (next_latent, denoised)


def solution(mesh):
    in_specs = (
        P("cfg", ("seq", "head"), None),
        P("cfg", ("seq", "head"), None),
        P("cfg", ("seq", "head"), None),
        P("cfg", None, None),
        P("cfg", None, None),
        P("cfg"),
        P(),
        P("cfg", ("seq", "head"), None),
        P("head", None),
        P(),
        P("cfg", None),
        P("cfg", None),
        P(),
        P("cfg", ("seq", "head")),
        P(),
    )
    out_specs = (P("cfg", ("seq", "head")), P("cfg", ("seq", "head")))
    return jax.shard_map(shards, mesh=mesh, in_specs=in_specs, out_specs=out_specs, check_vma=False)
```

```python
import functools

import jax
import jax.numpy as jnp
from jax import lax
from jax.experimental import pallas as pl
from jax.experimental.pallas import tpu as pltpu
from jax.sharding import PartitionSpec as P

HDIM = 64
STEPS = 28
GUIDANCE = 3.5
GROUP_HEADS = 5
FEATURES = 320
TOKENS = 128
SLOTS = 384
QUERIES = 1024
TILE = 256
SCORE_SCALE = 0.125 * 1.4426950408889634
MESH = pl.DeviceIdType.MESH
f32 = jnp.float32
bf16 = jnp.bfloat16


def sigma_at(position):
    level = 1.0 - position.astype(jnp.float32) / STEPS
    return 3.0 * level / (1.0 + 2.0 * level)


def block_kernel(
    q_hbm,
    k_hbm,
    v_hbm,
    tk_hbm,
    tv_hbm,
    w_hbm,
    hidden_hbm,
    len_hbm,
    mask_hbm,
    bias_hbm,
    shift_hbm,
    scale_hbm,
    final_hbm,
    guided_ref,
    loaded,
    text_slab,
    q_stage,
    kv_stage,
    o_stage,
    q_recv,
    o_recv,
    kv,
    weight,
    qx,
    text_keys,
    text_values,
    s0,
    s1,
    p0,
    p1,
    m_ref,
    acc,
    hidden,
    attended,
    residual,
    v_stage,
    v_recv,
    len_ref,
    mask_ref,
    out_bias,
    shift_ref,
    scale_ref,
    final_weight,
    load_sem,
    q_send,
    q_recv_sem,
    a_send,
    a_recv,
    b_send,
    b_recv,
    c_send,
    c_recv,
    o_send,
    o_recv_sem,
    w_send,
    w_recv,
    v_sem,
):
    cfg = lax.axis_index("cfg")
    seq = lax.axis_index("seq")
    group = lax.axis_index("head")
    core = lax.rem(seq, 2)
    parity = lax.rem(group, 2)
    row = group // 2
    right = lax.rem(seq + 2, 8)
    left = lax.rem(seq + 6, 8)
    sibling = seq + 1 - 2 * core
    far = lax.rem(seq + 2 + 4 * core, 8)
    turned = group + 1 - 2 * parity
    w_right = lax.rem(group + 2, 8)
    w_left = lax.rem(group + 6, 8)
    w_opposite = lax.rem(group + 4, 8)
    w_far = lax.rem(group + 2 + 4 * core, 8)

    slab_start = pl.multiple_of(128 * ((5 * group) // 2), 128)
    loads = (
        [
            pltpu.make_async_copy(src.at[0], loaded.at[i], load_sem.at[i])
            for i, src in enumerate((q_hbm, k_hbm, v_hbm))
        ]
        + [
            pltpu.make_async_copy(
                src.at[0, :, pl.ds(slab_start, 384)], text_slab.at[i], load_sem.at[3 + i]
            )
            for i, src in enumerate((tk_hbm, tv_hbm))
        ]
        + [
            pltpu.make_async_copy(
                w_hbm.at[pl.ds(160 * i, 160)], weight.at[2 * group + i], load_sem.at[5 + i]
            )
            for i in range(2)
        ]
        + [pltpu.make_async_copy(hidden_hbm.at[0], hidden, load_sem.at[7])]
        + [
            pltpu.make_async_copy(src, dst, load_sem.at[8 + i])
            for i, (src, dst) in enumerate(
                (
                    (bias_hbm, out_bias),
                    (shift_hbm, shift_ref),
                    (scale_hbm, scale_ref),
                    (final_hbm, final_weight),
                    (mask_hbm, mask_ref),
                    (len_hbm, len_ref),
                )
            )
        ]
    )
    for load in loads:
        load.start()

    barrier = pltpu.get_barrier_semaphore()
    for d in range(1, 8):
        pl.semaphore_signal(
            barrier, inc=1, device_id={"head": lax.rem(group + d, 8)}, device_id_type=MESH
        )
    for near in (right, left, sibling):
        pl.semaphore_signal(barrier, inc=1, device_id={"seq": near}, device_id_type=MESH)
    pl.semaphore_signal(barrier, inc=1, device_id={"cfg": 1 - cfg}, device_id_type=MESH)
    pl.semaphore_signal(
        barrier, inc=1, device_id={"cfg": 1 - cfg, "head": turned}, device_id_type=MESH
    )

    low = lax.broadcasted_iota(jnp.int32, (TOKENS, 128), 1) < HDIM
    low_half = lax.broadcasted_iota(jnp.int32, (HDIM, 128), 1) < HDIM

    loads[0].wait()
    for i in range(20):
        block = loaded[0, :, 128 * i : 128 * (i + 1)].T
        for half in range(2):
            f = 128 * i + HDIM * half
            q_stage[f // FEATURES, pl.ds(f % FEATURES, HDIM), :] = block[
                HDIM * half : HDIM * (half + 1)
            ]
    pl.semaphore_wait(barrier, 12)

    def head_copy(src, dst, send, recv, d):
        peer = lax.rem(group + d, 8)
        return pltpu.make_async_remote_copy(
            src_ref=src.at[peer],
            dst_ref=dst.at[0 if isinstance(d, int) else 1, row],
            send_sem=send.at[d],
            recv_sem=recv.at[d],
            device_id={"head": peer},
            device_id_type=MESH,
        )

    def q_copy(d):
        return head_copy(q_stage, q_recv, q_send, q_recv_sem, d)

    def kv_copy(d):
        return head_copy(kv_stage, kv, a_send, a_recv, d)

    along = (2, 6, 4)
    across = [lax.rem(1 + 2 * k + 6 * parity, 8) for k in range(4)]
    for d in along:
        q_copy(d).start()
    for d in across:
        q_copy(d).start()
    q_recv[0, pl.ds(row, 1)] = q_stage[pl.ds(group, 1)]

    loads[1].wait()
    loads[2].wait()
    for p in range(8):
        first = (5 * p) // 2
        tiles = [
            loaded[1, :, 128 * (first + i) : 128 * (first + i + 1)].astype(f32) for i in range(3)
        ]
        if p % 2 == 0:
            kv_stage[p, 0:128, :] = tiles[0].astype(bf16)
            kv_stage[p, 128:256, :] = tiles[1].astype(bf16)
            last = jnp.where(low_half, tiles[2][:HDIM], pltpu.roll(tiles[2][HDIM:], HDIM, 1))
        else:
            kv_stage[p, 0:128, :] = jnp.where(low, tiles[1], tiles[0]).astype(bf16)
            kv_stage[p, 128:256, :] = jnp.where(low, tiles[2], tiles[1]).astype(bf16)
            last = jnp.where(low_half, pltpu.roll(tiles[2][:HDIM], HDIM, 1), tiles[2][HDIM:])
        kv_stage[p, 256:320, :] = last.astype(bf16)
    for i in range(20):
        block = loaded[2, :, 128 * i : 128 * (i + 1)].T
        for half in range(2):
            f = 128 * i + HDIM * half
            kv_stage[f // FEATURES, pl.ds(FEATURES + f % FEATURES, HDIM), :] = block[
                HDIM * half : HDIM * (half + 1)
            ]
    for d in along:
        kv_copy(d).start()
    kv_copy(across[0]).start()
    kv[0, pl.ds(row, 1)] = kv_stage[pl.ds(group, 1)]

    def block_copy(k, d):
        at = lax.rem(group + 8 - d, 8) // 2
        return pltpu.make_async_remote_copy(
            src_ref=kv.at[k // 4, at],
            dst_ref=kv.at[2 + k // 4, at],
            send_sem=c_send.at[k],
            recv_sem=c_recv.at[k],
            device_id={"seq": sibling},
            device_id_type=MESH,
        )

    blocks = [block_copy(k, d) for k, d in enumerate((0, *along, *across))]
    blocks[0].start()

    loads[3].wait()
    loads[4].wait()
    odd = parity == 1
    swap = jnp.logical_and(lax.broadcasted_iota(jnp.int32, (SLOTS, 128), 1) < HDIM, odd)
    slabs = [text_slab[0, :, 128 * i : 128 * (i + 1)].astype(f32) for i in range(3)]
    text_keys[0] = jnp.where(swap, slabs[1], slabs[0]).astype(bf16)
    text_keys[1] = jnp.where(swap, slabs[2], slabs[1]).astype(bf16)
    text_keys[2] = slabs[2].astype(bf16)
    for i in range(3):
        for j in range(3):
            text_values[128 * i : 128 * (i + 1), 128 * j : 128 * (j + 1)] = text_slab[
                1, 128 * j : 128 * (j + 1), 128 * i : 128 * (i + 1)
            ].T

    zero = jnp.zeros((HDIM, TILE), bf16)
    ones = jnp.ones((16, 512), bf16)

    def queries_and_text(t, _):
        dead = lax.broadcasted_iota(jnp.int32, (SLOTS, TILE), 0) >= len_ref[0]
        for h in range(GROUP_HEADS):
            rows = slice(HDIM * h, HDIM * (h + 1))
            q = jnp.concatenate(
                [q_recv[t // 2, 2 * (t % 2), rows], q_recv[t // 2, 2 * (t % 2) + 1, rows]], 1
            )
            if h < 4:
                offset = parity if h % 2 == 0 else 1 - parity
                qx[6 * t + h, pl.ds(pl.multiple_of(HDIM * offset, HDIM), HDIM), :] = q
                qx[6 * t + h, pl.ds(pl.multiple_of(HDIM * (1 - offset), HDIM), HDIM), :] = zero
            else:
                for side in range(2):
                    qx[6 * t + 4 + side, HDIM * side : HDIM * (side + 1), :] = q
                    qx[6 * t + 4 + side, HDIM * (1 - side) : HDIM * (2 - side), :] = zero
        for h in range(GROUP_HEADS):
            weights_at = 6 * t + h if h < 4 else 6 * t + 4 + parity
            s = jnp.dot(text_keys[h // 2], qx[weights_at], preferred_element_type=f32)
            s = jnp.where(dead, -1e30, s)
            top = jnp.max(s, axis=0, keepdims=True)
            p = jnp.exp2((s - top) * SCORE_SCALE).astype(bf16)
            values = text_values[pl.ds(pl.multiple_of(HDIM * (parity + h), HDIM), HDIM), :]
            acc[GROUP_HEADS * t + h] = jnp.dot(
                jnp.concatenate([values, ones[:, :SLOTS]], 0), p, preferred_element_type=f32
            )
            m_ref[GROUP_HEADS * t + h] = top
        return 0

    loads[13].wait()
    for d in (*along, *across):
        q_copy(d).wait_recv()
    lax.fori_loop(0, 4, queries_and_text, 0)

    def ring_copy(k, src, dst, target):
        return pltpu.make_async_remote_copy(
            src_ref=kv.at[src],
            dst_ref=kv.at[dst],
            send_sem=b_send.at[k],
            recv_sem=b_recv.at[dst],
            device_id={"seq": target},
            device_id_type=MESH,
        )

    copies = {
        0: (ring_copy(0, 0, 4, right), ring_copy(1, 0, 5, left)),
        1: (ring_copy(2, 1, 8, right), ring_copy(3, 1, 9, left)),
        2: (ring_copy(4, 4, 6, sibling), ring_copy(5, 5, 7, sibling)),
        3: (ring_copy(6, 4 + core, 12, far),),
        4: (ring_copy(7, 8 + core, 14, far), ring_copy(8, 8, 10, sibling), ring_copy(9, 9, 11, sibling)),
        5: (ring_copy(10, 12, 13, sibling), ring_copy(11, 14, 15, sibling)),
    }

    def arrived(*slots):
        for dst in slots:
            ring_copy(0, dst, dst, sibling).wait_recv()

    def send(stage):
        for copy in copies[stage]:
            copy.start()

    def weight_copy(k, owner, target, from_hbm=False):
        at = 2 * owner + core
        return pltpu.make_async_remote_copy(
            src_ref=w_hbm.at[pl.ds(pl.multiple_of(160 * core, 160), 160)] if from_hbm else weight.at[at],
            dst_ref=weight.at[at],
            send_sem=w_send.at[k],
            recv_sem=w_recv.at[k],
            device_id=target,
            device_id_type=MESH,
        )

    to_right, to_left = {"head": w_right}, {"head": w_left}
    to_turned = {"cfg": 1 - cfg, "head": turned}
    to_sibling = {"seq": sibling}
    owners = (
        w_left,
        w_right,
        turned,
        w_opposite,
        lax.rem(turned + 6, 8),
        lax.rem(turned + 2, 8),
        lax.rem(turned + 4, 8),
    )
    weight_copies = {
        0: (
            weight_copy(0, group, to_right, True),
            weight_copy(1, group, to_left, True),
            weight_copy(2, group, to_turned, True),
        ),
        1: (weight_copy(3, lax.rem(group + 6 + 4 * core, 8), {"head": w_far}),),
        2: (
            weight_copy(6, w_opposite, to_turned),
            weight_copy(4, turned, to_right),
            weight_copy(5, turned, to_left),
        ),
    }
    to_core = [weight_copy(7 + k, owners[k], to_sibling) for k in range(7)]

    def weight_arrived(*which):
        for k in which:
            weight_copy(k, group, to_sibling).wait_recv()

    def weight_send(stage):
        for copy in weight_copies[stage]:
            copy.start()

    def share(*which):
        for k in which:
            to_core[k].start()

    s_bufs = (s0, s1)
    p_bufs = (p0, p1)

    def score_parts(step, r, t, h, buf):
        for side in range(2):
            slot = step[side]
            if h < 4:
                for first in range(0, 4, 2):
                    lhs = jnp.concatenate(
                        [kv[slot, b, 128 * (h // 2) : 128 * (h // 2 + 1), :] for b in range(first, first + 2)], 0
                    )
                    s = jnp.dot(lhs, qx[6 * t + h], preferred_element_type=f32)
                    at = 512 * side + 128 * first
                    buf[at : at + 128 * 2, :] = s
                    yield jnp.max(s.reshape(16 * 2, 8, TILE), axis=0)
            else:
                lhs = jnp.concatenate([kv[slot, b, 256:320, :] for b in range(4)], 0)
                for half in range(2):
                    s = jnp.dot(lhs, qx[6 * t + 4 + half], preferred_element_type=f32)
                    for b in range(4):
                        at = 512 * side + 128 * b + HDIM * half
                        buf[at : at + HDIM, :] = s[HDIM * b : HDIM * (b + 1)]
                    yield jnp.max(s.reshape(32, 8, TILE), axis=0)

    def weigh_parts(buf, top, out):
        for j in range(0, QUERIES, 256):
            out[j : j + 256, :] = jnp.exp2((buf[j : j + 256, :] - top) * SCORE_SCALE).astype(bf16)
            yield None

    def value_parts(step, r, h, buf):
        for side in range(2):
            slot = step[side]
            rows = FEATURES + HDIM * h
            lhs = jnp.concatenate([kv[slot, b, rows : rows + HDIM, :] for b in range(4)], 1)
            yield jnp.dot(
                jnp.concatenate([lhs, ones], 0),
                buf[512 * side : 512 * (side + 1), :],
                preferred_element_type=f32,
            )

    def woven(*streams):
        given = [[] for _ in streams]
        waiting = [list_of for list_of in streams]
        live = list(range(len(streams)))
        while live:
            for i in tuple(live):
                try:
                    given[i].append(next(waiting[i]))
                except StopIteration:
                    live.remove(i)
        return given

    def new_top(r, parts):
        best = functools.reduce(jnp.maximum, parts)
        old = m_ref[r]
        new = jnp.maximum(old, jnp.max(best, axis=0, keepdims=True))
        m_ref[r] = new
        return new, jnp.exp2((old - new) * SCORE_SCALE)

    def finish(t, _):
        for h in range(GROUP_HEADS):
            sums = acc[GROUP_HEADS * t + h]
            gain = mask_ref[GROUP_HEADS * group + h].astype(f32)
            out = (sums[:HDIM] / sums[HDIM : HDIM + 1] * gain).astype(bf16)
            for side in range(2):
                o_stage[t // 2, 2 * (t % 2) + side, HDIM * h : HDIM * (h + 1), :] = out[
                    :, 128 * side : 128 * (side + 1)
                ]
        return 0

    def o_copy(d):
        peer = lax.rem(group + d, 8)
        return pltpu.make_async_remote_copy(
            src_ref=o_stage.at[0 if isinstance(d, int) else 1, peer // 2],
            dst_ref=o_recv.at[group],
            send_sem=o_send.at[d],
            recv_sem=o_recv_sem.at[d],
            device_id={"head": peer},
            device_id_type=MESH,
        )

    def at_start(half):
        @pl.when(half == 0)
        def _():
            for k, d in enumerate(along):
                kv_copy(d).wait_recv()
                blocks[1 + k].start()
            send(0)
            for d in across[1:]:
                kv_copy(d).start()
            for block in blocks[:4]:
                block.wait_recv()

        @pl.when(half == 2)
        def _():
            for k, d in enumerate(across):
                kv_copy(d).wait_recv()
                blocks[4 + k].start()
            send(1)
            weight_send(0)
            for block in blocks[4:]:
                block.wait_recv()

        @pl.when(half == 4)
        def _():
            arrived(4, 5)
            send(2)

        @pl.when(half == 6)
        def _():
            arrived(6, 7)
            send(3)

        @pl.when(half == 7)
        def _():
            weight_arrived(0, 1, 2)
            weight_send(1)
            share(0, 1, 2)

        @pl.when(half == 8)
        def _():
            arrived(8, 9)
            send(4)

        @pl.when(half == 10)
        def _():
            arrived(10, 11)
            weight_arrived(3)
            weight_send(2)
            share(3)

        @pl.when(half == 12)
        def _():
            arrived(12, 14)
            send(5)

        @pl.when(half == 14)
        def _():
            arrived(13, 15)

        @pl.when(half == 15)
        def _():
            loads[12].wait()
            lax.fori_loop(2, 4, finish, 0)
            for d in across:
                o_copy(d).start()

    def half_step(half, _):
        at_start(half)
        order = half // 2
        one = jnp.where(order < 2, order, jnp.where(order < 6, 2 * order, order + 6))
        two = jnp.where(order < 2, order + 2, jnp.where(order < 6, 2 * order + 1, order + 8))
        side = jnp.where(order == 7, 1 - half % 2, half % 2)
        where = (one, two)

        def unit(j):
            return 10 * side + j, 2 * side + j // 5, j % 5

        (parts,) = woven(score_parts(where, *unit(0), s0))
        top, rescale = new_top(unit(0)[0], parts)
        before = None
        for j in range(10):
            streams = [weigh_parts(s_bufs[j % 2], top, p_bufs[j % 2])]
            if j < 9:
                streams.insert(0, score_parts(where, *unit(j + 1), s_bufs[(j + 1) % 2]))
            if j > 0:
                r, _, h = unit(j - 1)
                streams.append(value_parts(where, r, h, p_bufs[(j + 1) % 2]))
            given = woven(*streams)
            if j > 0:
                acc[r] = acc[r] * before + functools.reduce(jnp.add, given[-1])
            before = rescale
            if j < 9:
                top, rescale = new_top(unit(j + 1)[0], given[0])
        r, _, h = unit(9)
        (given,) = woven(value_parts(where, r, h, p1))
        acc[r] = acc[r] * before + functools.reduce(jnp.add, given)
        return 0

    lax.fori_loop(0, 16, half_step, 0)

    lax.fori_loop(0, 2, finish, 0)
    for d in along:
        o_copy(d).start()
    weight_arrived(4, 5, 6)
    share(4, 5, 6)
    o_recv[pl.ds(group, 1)] = o_stage[0, pl.ds(row, 1)]

    for d in (*along, *across):
        q_copy(d).wait_send()
        kv_copy(d).wait_send()
    for block in blocks:
        block.wait_send()
    for stage in copies.values():
        for copy in stage:
            copy.wait_send()
    for stage in weight_copies.values():
        for copy in stage:
            copy.wait_send()

    for d in (*across, *along):
        o_copy(d).wait_recv()
    for p in range(8):
        for h in range(GROUP_HEADS):
            f = FEATURES * p + HDIM * h
            if f % 128 == 0:
                q = f // 128
                lo = o_recv[p, HDIM * h : HDIM * (h + 1), :]
                nxt = f + HDIM
                hi = o_recv[nxt // FEATURES, nxt % FEATURES : nxt % FEATURES + HDIM, :]
                attended[:, 128 * q : 128 * (q + 1)] = jnp.concatenate([lo, hi], 0).T
    for load in loads[5:12]:
        load.wait()
    weight_arrived(7, 8, 9, 10, 11, 12, 13)
    rows = attended[...]
    width = 2432
    total = None
    for n in range(0, width, TILE):
        cols = slice(n, min(n + TILE, width))
        part = jnp.dot(
            rows,
            jnp.concatenate([weight[i, :, cols] for i in range(16)], 0),
            preferred_element_type=f32,
        )
        part = hidden[:, cols].astype(f32) + part + out_bias[cols].astype(f32).reshape(1, -1)
        residual[:, cols] = part
        part = jnp.sum(part, axis=1, keepdims=True)
        total = part if total is None else total + part
    centre = total / width
    total = None
    for n in range(0, width, TILE):
        cols = slice(n, min(n + TILE, width))
        part = residual[:, cols] - centre
        residual[:, cols] = part
        part = jnp.sum(part * part, axis=1, keepdims=True)
        total = part if total is None else total + part
    norm = 1.0 / jnp.sqrt(total / width + 1e-06)
    velocity = None
    for n in range(0, width, TILE):
        cols = slice(n, min(n + TILE, width))
        modulated = residual[:, cols] * norm * (1.0 + scale_ref[:, cols].astype(f32)) + shift_ref[
            :, cols
        ].astype(f32)
        part = lax.dot_general(
            final_weight[:, cols],
            modulated.astype(bf16),
            (((1,), (1,)), ((), ())),
            preferred_element_type=f32,
        )
        velocity = part if velocity is None else velocity + part
    v_stage[0] = velocity[:32].astype(bf16)
    v_stage[1] = velocity[32:].astype(bf16)
    exchange = pltpu.make_async_remote_copy(
        src_ref=v_stage.at[1 - cfg],
        dst_ref=v_recv,
        send_sem=v_sem.at[0],
        recv_sem=v_sem.at[1],
        device_id={"cfg": 1 - cfg},
        device_id_type=MESH,
    )
    exchange.start()
    mine = jnp.where(cfg == 0, velocity[:32], velocity[32:])
    for d in (*along, *across):
        o_copy(d).wait_send()
    for copy in to_core:
        copy.wait_send()
    exchange.wait()
    theirs = v_recv[...].astype(f32)
    cond = jnp.where(cfg == 0, mine, theirs)
    uncond = jnp.where(cfg == 0, theirs, mine)
    guided_ref[...] = uncond + GUIDANCE * (cond - uncond)


def shards(
    q_img,
    k_img,
    v_img,
    text_k,
    text_v,
    text_len,
    head_mask,
    hidden,
    out_weight,
    out_bias,
    final_shift,
    final_scale,
    final_weight,
    latent,
    step_index,
):
    vmem = pltpu.VMEM
    dma = pltpu.SemaphoreType.DMA
    anywhere = pl.BlockSpec(memory_space=pl.ANY)
    whole = pl.BlockSpec(memory_space=pltpu.VMEM)
    guided = pl.pallas_call(
        block_kernel,
        out_shape=jax.ShapeDtypeStruct(latent.shape, f32),
        in_specs=[anywhere] * 13,
        out_specs=whole,
        scratch_shapes=[
            vmem((3, TOKENS, 2560), bf16),
            vmem((2, SLOTS, 384), bf16),
            vmem((8, FEATURES, TOKENS), bf16),
            vmem((8, 2 * FEATURES, TOKENS), bf16),
            vmem((2, 4, FEATURES, TOKENS), bf16),
            vmem((2, 4, FEATURES, TOKENS), bf16),
            vmem((8, FEATURES, TOKENS), bf16),
            vmem((16, 4, 2 * FEATURES, TOKENS), bf16),
            vmem((16, 160, 2432), bf16),
            vmem((24, 128, TILE), bf16),
            vmem((3, SLOTS, 128), bf16),
            vmem((384, SLOTS), bf16),
            vmem((QUERIES, TILE), f32),
            vmem((QUERIES, TILE), f32),
            vmem((QUERIES, TILE), bf16),
            vmem((QUERIES, TILE), bf16),
            vmem((20, 1, TILE), f32),
            vmem((20, 80, TILE), f32),
            vmem((TOKENS, 2432), bf16),
            vmem((TOKENS, 2560), bf16),
            vmem((TOKENS, 2432), f32),
            vmem((2, 32, TOKENS), bf16),
            vmem((32, TOKENS), bf16),
            pltpu.SMEM((1,), jnp.int32),
            pltpu.SMEM((40,), jnp.int32),
            vmem((2432,), bf16),
            vmem((1, 2432), bf16),
            vmem((1, 2432), bf16),
            vmem((64, 2432), bf16),
            dma((14,)),
            dma((8,)),
            dma((8,)),
            dma((8,)),
            dma((8,)),
            dma((12,)),
            dma((16,)),
            dma((8,)),
            dma((8,)),
            dma((8,)),
            dma((8,)),
            dma((14,)),
            dma((14,)),
            dma((2,)),
        ],
        compiler_params=pltpu.CompilerParams(
            collective_id=0, has_side_effects=True, vmem_limit_bytes=60 << 20
        ),
        cost_estimate=pl.CostEstimate(
            flops=40_000_000_000, bytes_accessed=20_000_000, transcendentals=44_000_000
        ),
    )(
        q_img,
        k_img,
        v_img,
        text_k,
        text_v,
        out_weight,
        hidden,
        text_len,
        head_mask,
        out_bias,
        final_shift,
        final_scale,
        final_weight,
    )
    sigma_now = sigma_at(step_index[0])
    sigma_next = sigma_at(step_index[0] + 1)
    denoised = latent - sigma_now * guided
    next_latent = latent + (sigma_next - sigma_now) * guided
    return (next_latent, denoised)


def solution(mesh):
    in_specs = (
        P("cfg", ("seq", "head"), None),
        P("cfg", ("seq", "head"), None),
        P("cfg", ("seq", "head"), None),
        P("cfg", None, None),
        P("cfg", None, None),
        P("cfg"),
        P(),
        P("cfg", ("seq", "head"), None),
        P("head", None),
        P(),
        P("cfg", None),
        P("cfg", None),
        P(),
        P("cfg", ("seq", "head")),
        P(),
    )
    out_specs = (P("cfg", ("seq", "head")), P("cfg", ("seq", "head")))
    return jax.shard_map(shards, mesh=mesh, in_specs=in_specs, out_specs=out_specs, check_vma=False)
```

```python
import functools

import jax
import jax.numpy as jnp
from jax import lax
from jax.experimental import pallas as pl
from jax.experimental.pallas import tpu as pltpu
from jax.sharding import PartitionSpec as P

HDIM = 64
STEPS = 28
GUIDANCE = 3.5
GROUP_HEADS = 5
FEATURES = 320
TOKENS = 128
SLOTS = 384
QUERIES = 1024
TILE = 256
SCORE_SCALE = 0.125 * 1.4426950408889634
MESH = pl.DeviceIdType.MESH
f32 = jnp.float32
bf16 = jnp.bfloat16


def sigma_at(position):
    level = 1.0 - position.astype(jnp.float32) / STEPS
    return 3.0 * level / (1.0 + 2.0 * level)


def block_kernel(
    q_hbm,
    k_hbm,
    v_hbm,
    tk_hbm,
    tv_hbm,
    w_hbm,
    hidden_hbm,
    len_hbm,
    mask_hbm,
    bias_hbm,
    shift_hbm,
    scale_hbm,
    final_hbm,
    guided_ref,
    loaded,
    text_slab,
    q_stage,
    kv_stage,
    o_stage,
    q_recv,
    o_recv,
    kv,
    weight,
    qx,
    text_keys,
    text_values,
    s0,
    s1,
    p0,
    p1,
    m_ref,
    acc,
    hidden,
    attended,
    residual,
    v_stage,
    v_recv,
    len_ref,
    mask_ref,
    out_bias,
    shift_ref,
    scale_ref,
    final_weight,
    load_sem,
    q_send,
    q_recv_sem,
    a_send,
    a_recv,
    b_send,
    b_recv,
    c_send,
    c_recv,
    o_send,
    o_recv_sem,
    w_send,
    w_recv,
    v_sem,
):
    cfg = lax.axis_index("cfg")
    seq = lax.axis_index("seq")
    group = lax.axis_index("head")
    core = lax.rem(seq, 2)
    parity = lax.rem(group, 2)
    row = group // 2
    right = lax.rem(seq + 2, 8)
    left = lax.rem(seq + 6, 8)
    sibling = seq + 1 - 2 * core
    far = lax.rem(seq + 2 + 4 * core, 8)
    turned = group + 1 - 2 * parity
    w_right = lax.rem(group + 2, 8)
    w_left = lax.rem(group + 6, 8)
    w_opposite = lax.rem(group + 4, 8)
    w_far = lax.rem(group + 2 + 4 * core, 8)

    slab_start = pl.multiple_of(128 * ((5 * group) // 2), 128)
    loads = (
        [
            pltpu.make_async_copy(src.at[0], loaded.at[i], load_sem.at[i])
            for i, src in enumerate((q_hbm, k_hbm, v_hbm))
        ]
        + [
            pltpu.make_async_copy(
                src.at[0, :, pl.ds(slab_start, 384)], text_slab.at[i], load_sem.at[3 + i]
            )
            for i, src in enumerate((tk_hbm, tv_hbm))
        ]
        + [
            pltpu.make_async_copy(
                w_hbm.at[pl.ds(160 * i, 160)], weight.at[2 * group + i], load_sem.at[5 + i]
            )
            for i in range(2)
        ]
        + [pltpu.make_async_copy(hidden_hbm.at[0], hidden, load_sem.at[7])]
        + [
            pltpu.make_async_copy(src, dst, load_sem.at[8 + i])
            for i, (src, dst) in enumerate(
                (
                    (bias_hbm, out_bias),
                    (shift_hbm, shift_ref),
                    (scale_hbm, scale_ref),
                    (final_hbm, final_weight),
                    (mask_hbm, mask_ref),
                    (len_hbm, len_ref),
                )
            )
        ]
    )
    for load in loads:
        load.start()

    barrier = pltpu.get_barrier_semaphore()
    for d in range(1, 8):
        pl.semaphore_signal(
            barrier, inc=1, device_id={"head": lax.rem(group + d, 8)}, device_id_type=MESH
        )
    for near in (right, left, sibling):
        pl.semaphore_signal(barrier, inc=1, device_id={"seq": near}, device_id_type=MESH)
    pl.semaphore_signal(barrier, inc=1, device_id={"cfg": 1 - cfg}, device_id_type=MESH)
    pl.semaphore_signal(
        barrier, inc=1, device_id={"cfg": 1 - cfg, "head": turned}, device_id_type=MESH
    )

    low = lax.broadcasted_iota(jnp.int32, (TOKENS, 128), 1) < HDIM
    low_half = lax.broadcasted_iota(jnp.int32, (HDIM, 128), 1) < HDIM

    loads[0].wait()
    for i in range(20):
        block = loaded[0, :, 128 * i : 128 * (i + 1)].T
        for half in range(2):
            f = 128 * i + HDIM * half
            q_stage[f // FEATURES, pl.ds(f % FEATURES, HDIM), :] = block[
                HDIM * half : HDIM * (half + 1)
            ]
    pl.semaphore_wait(barrier, 12)

    def head_copy(src, dst, send, recv, d):
        peer = lax.rem(group + d, 8)
        return pltpu.make_async_remote_copy(
            src_ref=src.at[peer],
            dst_ref=dst.at[0 if isinstance(d, int) else 1, row],
            send_sem=send.at[d],
            recv_sem=recv.at[d],
            device_id={"head": peer},
            device_id_type=MESH,
        )

    def q_copy(d):
        return head_copy(q_stage, q_recv, q_send, q_recv_sem, d)

    def kv_copy(d):
        return head_copy(kv_stage, kv, a_send, a_recv, d)

    along = (2, 6, 4)
    across = [lax.rem(1 + 2 * k + 6 * parity, 8) for k in range(4)]
    for d in (4, 2, 6):
        q_copy(d).start()
    for d in across:
        q_copy(d).start()
    q_recv[0, pl.ds(row, 1)] = q_stage[pl.ds(group, 1)]

    loads[1].wait()
    loads[2].wait()
    for p in range(8):
        first = (5 * p) // 2
        tiles = [
            loaded[1, :, 128 * (first + i) : 128 * (first + i + 1)].astype(f32) for i in range(3)
        ]
        if p % 2 == 0:
            kv_stage[p, 0:128, :] = tiles[0].astype(bf16)
            kv_stage[p, 128:256, :] = tiles[1].astype(bf16)
            last = jnp.where(low_half, tiles[2][:HDIM], pltpu.roll(tiles[2][HDIM:], HDIM, 1))
        else:
            kv_stage[p, 0:128, :] = jnp.where(low, tiles[1], tiles[0]).astype(bf16)
            kv_stage[p, 128:256, :] = jnp.where(low, tiles[2], tiles[1]).astype(bf16)
            last = jnp.where(low_half, pltpu.roll(tiles[2][:HDIM], HDIM, 1), tiles[2][HDIM:])
        kv_stage[p, 256:320, :] = last.astype(bf16)
    for i in range(20):
        block = loaded[2, :, 128 * i : 128 * (i + 1)].T
        for half in range(2):
            f = 128 * i + HDIM * half
            kv_stage[f // FEATURES, pl.ds(FEATURES + f % FEATURES, HDIM), :] = block[
                HDIM * half : HDIM * (half + 1)
            ]
    for d in (4, 2, 6):
        kv_copy(d).start()
    kv_copy(across[0]).start()
    kv[0, pl.ds(row, 1)] = kv_stage[pl.ds(group, 1)]

    def block_copy(k, d):
        at = lax.rem(group + 8 - d, 8) // 2
        return pltpu.make_async_remote_copy(
            src_ref=kv.at[k // 4, at],
            dst_ref=kv.at[2 + k // 4, at],
            send_sem=c_send.at[k],
            recv_sem=c_recv.at[k],
            device_id={"seq": sibling},
            device_id_type=MESH,
        )

    blocks = [block_copy(k, d) for k, d in enumerate((0, *along, *across))]
    blocks[0].start()

    loads[3].wait()
    loads[4].wait()
    odd = parity == 1
    swap = jnp.logical_and(lax.broadcasted_iota(jnp.int32, (SLOTS, 128), 1) < HDIM, odd)
    slabs = [text_slab[0, :, 128 * i : 128 * (i + 1)].astype(f32) for i in range(3)]
    text_keys[0] = jnp.where(swap, slabs[1], slabs[0]).astype(bf16)
    text_keys[1] = jnp.where(swap, slabs[2], slabs[1]).astype(bf16)
    text_keys[2] = slabs[2].astype(bf16)
    for i in range(3):
        for j in range(3):
            text_values[128 * i : 128 * (i + 1), 128 * j : 128 * (j + 1)] = text_slab[
                1, 128 * j : 128 * (j + 1), 128 * i : 128 * (i + 1)
            ].T

    zero = jnp.zeros((HDIM, TILE), bf16)
    ones = jnp.ones((16, 512), bf16)

    def queries_and_text(t, _):
        dead = lax.broadcasted_iota(jnp.int32, (SLOTS, TILE), 0) >= len_ref[0]
        for h in range(GROUP_HEADS):
            rows = slice(HDIM * h, HDIM * (h + 1))
            q = jnp.concatenate(
                [q_recv[t // 2, 2 * (t % 2), rows], q_recv[t // 2, 2 * (t % 2) + 1, rows]], 1
            )
            if h < 4:
                offset = parity if h % 2 == 0 else 1 - parity
                qx[6 * t + h, pl.ds(pl.multiple_of(HDIM * offset, HDIM), HDIM), :] = q
                qx[6 * t + h, pl.ds(pl.multiple_of(HDIM * (1 - offset), HDIM), HDIM), :] = zero
            else:
                for side in range(2):
                    qx[6 * t + 4 + side, HDIM * side : HDIM * (side + 1), :] = q
                    qx[6 * t + 4 + side, HDIM * (1 - side) : HDIM * (2 - side), :] = zero
        for h in range(GROUP_HEADS):
            weights_at = 6 * t + h if h < 4 else 6 * t + 4 + parity
            s = jnp.dot(text_keys[h // 2], qx[weights_at], preferred_element_type=f32)
            s = jnp.where(dead, -1e30, s)
            top = jnp.max(s, axis=0, keepdims=True)
            p = jnp.exp2((s - top) * SCORE_SCALE).astype(bf16)
            values = text_values[pl.ds(pl.multiple_of(HDIM * (parity + h), HDIM), HDIM), :]
            acc[GROUP_HEADS * t + h] = jnp.dot(
                jnp.concatenate([values, ones[:, :SLOTS]], 0), p, preferred_element_type=f32
            )
            m_ref[GROUP_HEADS * t + h] = top
        return 0

    loads[13].wait()
    for d in along:
        q_copy(d).wait_recv()
    lax.fori_loop(0, 2, queries_and_text, 0)

    def ring_copy(k, src, dst, target):
        return pltpu.make_async_remote_copy(
            src_ref=kv.at[src],
            dst_ref=kv.at[dst],
            send_sem=b_send.at[k],
            recv_sem=b_recv.at[dst],
            device_id={"seq": target},
            device_id_type=MESH,
        )

    copies = {
        0: (ring_copy(0, 0, 4, right), ring_copy(1, 0, 5, left)),
        1: (ring_copy(2, 1, 8, right), ring_copy(3, 1, 9, left)),
        2: (ring_copy(4, 4, 6, sibling), ring_copy(5, 5, 7, sibling)),
        3: (ring_copy(6, 4 + core, 12, far),),
        4: (ring_copy(7, 8 + core, 14, far), ring_copy(8, 8, 10, sibling), ring_copy(9, 9, 11, sibling)),
        5: (ring_copy(10, 12, 13, sibling), ring_copy(11, 14, 15, sibling)),
    }

    def arrived(*slots):
        for dst in slots:
            ring_copy(0, dst, dst, sibling).wait_recv()

    def send(stage):
        for copy in copies[stage]:
            copy.start()

    def weight_copy(k, owner, target, from_hbm=False):
        at = 2 * owner + core
        return pltpu.make_async_remote_copy(
            src_ref=w_hbm.at[pl.ds(pl.multiple_of(160 * core, 160), 160)] if from_hbm else weight.at[at],
            dst_ref=weight.at[at],
            send_sem=w_send.at[k],
            recv_sem=w_recv.at[k],
            device_id=target,
            device_id_type=MESH,
        )

    to_right, to_left = {"head": w_right}, {"head": w_left}
    to_turned = {"cfg": 1 - cfg, "head": turned}
    to_sibling = {"seq": sibling}
    owners = (
        w_left,
        w_right,
        turned,
        w_opposite,
        lax.rem(turned + 6, 8),
        lax.rem(turned + 2, 8),
        lax.rem(turned + 4, 8),
    )
    weight_copies = {
        0: (
            weight_copy(0, group, to_right, True),
            weight_copy(1, group, to_left, True),
            weight_copy(2, group, to_turned, True),
        ),
        1: (weight_copy(3, lax.rem(group + 6 + 4 * core, 8), {"head": w_far}),),
        2: (
            weight_copy(6, w_opposite, to_turned),
            weight_copy(4, turned, to_right),
            weight_copy(5, turned, to_left),
        ),
    }
    to_core = [weight_copy(7 + k, owners[k], to_sibling) for k in range(7)]

    def weight_arrived(*which):
        for k in which:
            weight_copy(k, group, to_sibling).wait_recv()

    def weight_send(stage):
        for copy in weight_copies[stage]:
            copy.start()

    def share(*which):
        for k in which:
            to_core[k].start()

    s_bufs = (s0, s1)
    p_bufs = (p0, p1)

    def score_parts(step, r, t, h, buf):
        for side in range(2):
            slot = step[side]
            if h < 4:
                for first in range(0, 4, 2):
                    lhs = jnp.concatenate(
                        [kv[slot, b, 128 * (h // 2) : 128 * (h // 2 + 1), :] for b in range(first, first + 2)], 0
                    )
                    s = jnp.dot(lhs, qx[6 * t + h], preferred_element_type=f32)
                    at = 512 * side + 128 * first
                    buf[at : at + 128 * 2, :] = s
                    yield jnp.max(s.reshape(16 * 2, 8, TILE), axis=0)
            else:
                lhs = jnp.concatenate([kv[slot, b, 256:320, :] for b in range(4)], 0)
                for half in range(2):
                    s = jnp.dot(lhs, qx[6 * t + 4 + half], preferred_element_type=f32)
                    for b in range(4):
                        at = 512 * side + 128 * b + HDIM * half
                        buf[at : at + HDIM, :] = s[HDIM * b : HDIM * (b + 1)]
                    yield jnp.max(s.reshape(32, 8, TILE), axis=0)

    def weigh_parts(buf, top, out):
        for j in range(0, QUERIES, 256):
            out[j : j + 256, :] = jnp.exp2((buf[j : j + 256, :] - top) * SCORE_SCALE).astype(bf16)
            yield None

    def value_parts(step, r, h, buf):
        for side in range(2):
            slot = step[side]
            rows = FEATURES + HDIM * h
            lhs = jnp.concatenate([kv[slot, b, rows : rows + HDIM, :] for b in range(4)], 1)
            yield jnp.dot(
                jnp.concatenate([lhs, ones], 0),
                buf[512 * side : 512 * (side + 1), :],
                preferred_element_type=f32,
            )

    def woven(*streams):
        given = [[] for _ in streams]
        waiting = [list_of for list_of in streams]
        live = list(range(len(streams)))
        while live:
            for i in tuple(live):
                try:
                    given[i].append(next(waiting[i]))
                except StopIteration:
                    live.remove(i)
        return given

    def new_top(r, parts):
        best = functools.reduce(jnp.maximum, parts)
        old = m_ref[r]
        new = jnp.maximum(old, jnp.max(best, axis=0, keepdims=True))
        m_ref[r] = new
        return new, jnp.exp2((old - new) * SCORE_SCALE)

    def finish(t, _):
        for h in range(GROUP_HEADS):
            sums = acc[GROUP_HEADS * t + h]
            gain = mask_ref[GROUP_HEADS * group + h].astype(f32)
            out = (sums[:HDIM] / sums[HDIM : HDIM + 1] * gain).astype(bf16)
            for side in range(2):
                o_stage[t // 2, 2 * (t % 2) + side, HDIM * h : HDIM * (h + 1), :] = out[
                    :, 128 * side : 128 * (side + 1)
                ]
        return 0

    def o_copy(d):
        peer = lax.rem(group + d, 8)
        return pltpu.make_async_remote_copy(
            src_ref=o_stage.at[0 if isinstance(d, int) else 1, peer // 2],
            dst_ref=o_recv.at[group],
            send_sem=o_send.at[d],
            recv_sem=o_recv_sem.at[d],
            device_id={"head": peer},
            device_id_type=MESH,
        )

    def at_start(half):
        @pl.when(half == 0)
        def _():
            for k, d in enumerate(along):
                kv_copy(d).wait_recv()
                blocks[1 + k].start()
            send(0)
            for d in across[1:]:
                kv_copy(d).start()
            for block in blocks[:4]:
                block.wait_recv()

        @pl.when(half == 1)
        def _():
            for d in across:
                q_copy(d).wait_recv()
            lax.fori_loop(2, 4, queries_and_text, 0)

        @pl.when(half == 2)
        def _():
            for k, d in enumerate(across):
                kv_copy(d).wait_recv()
                blocks[4 + k].start()
            send(1)
            weight_send(0)
            for block in blocks[4:]:
                block.wait_recv()

        @pl.when(half == 4)
        def _():
            arrived(4, 5)
            send(2)

        @pl.when(half == 6)
        def _():
            arrived(6, 7)
            send(3)

        @pl.when(half == 7)
        def _():
            weight_arrived(0, 1, 2)
            weight_send(1)
            share(0, 1, 2)

        @pl.when(half == 8)
        def _():
            arrived(8, 9)
            send(4)

        @pl.when(half == 10)
        def _():
            arrived(10, 11)
            weight_arrived(3)
            weight_send(2)
            share(3)

        @pl.when(half == 12)
        def _():
            arrived(12, 14)
            send(5)

        @pl.when(half == 14)
        def _():
            arrived(13, 15)

        @pl.when(half == 15)
        def _():
            loads[12].wait()
            lax.fori_loop(2, 4, finish, 0)
            for d in across:
                o_copy(d).start()

    def half_step(half, _):
        at_start(half)
        order = half // 2
        one = jnp.where(order < 2, order, jnp.where(order < 6, 2 * order, order + 6))
        two = jnp.where(order < 2, order + 2, jnp.where(order < 6, 2 * order + 1, order + 8))
        side = jnp.where(order == 7, 1 - half % 2, half % 2)
        where = (one, two)

        def unit(j):
            return 10 * side + j, 2 * side + j // 5, j % 5

        (parts,) = woven(score_parts(where, *unit(0), s0))
        top, rescale = new_top(unit(0)[0], parts)
        before = None
        for j in range(10):
            streams = [weigh_parts(s_bufs[j % 2], top, p_bufs[j % 2])]
            if j < 9:
                streams.insert(0, score_parts(where, *unit(j + 1), s_bufs[(j + 1) % 2]))
            if j > 0:
                r, _, h = unit(j - 1)
                streams.append(value_parts(where, r, h, p_bufs[(j + 1) % 2]))
            given = woven(*streams)
            if j > 0:
                acc[r] = acc[r] * before + functools.reduce(jnp.add, given[-1])
            before = rescale
            if j < 9:
                top, rescale = new_top(unit(j + 1)[0], given[0])
        r, _, h = unit(9)
        (given,) = woven(value_parts(where, r, h, p1))
        acc[r] = acc[r] * before + functools.reduce(jnp.add, given)
        return 0

    lax.fori_loop(0, 16, half_step, 0)

    lax.fori_loop(0, 2, finish, 0)
    for d in along:
        o_copy(d).start()
    weight_arrived(4, 5, 6)
    share(4, 5, 6)
    o_recv[pl.ds(group, 1)] = o_stage[0, pl.ds(row, 1)]

    for d in (*along, *across):
        q_copy(d).wait_send()
        kv_copy(d).wait_send()
    for block in blocks:
        block.wait_send()
    for stage in copies.values():
        for copy in stage:
            copy.wait_send()
    for stage in weight_copies.values():
        for copy in stage:
            copy.wait_send()

    for d in (*across, *along):
        o_copy(d).wait_recv()
    for p in range(8):
        for h in range(GROUP_HEADS):
            f = FEATURES * p + HDIM * h
            if f % 128 == 0:
                q = f // 128
                lo = o_recv[p, HDIM * h : HDIM * (h + 1), :]
                nxt = f + HDIM
                hi = o_recv[nxt // FEATURES, nxt % FEATURES : nxt % FEATURES + HDIM, :]
                attended[:, 128 * q : 128 * (q + 1)] = jnp.concatenate([lo, hi], 0).T
    for load in loads[5:12]:
        load.wait()
    weight_arrived(7, 8, 9, 10, 11, 12, 13)
    rows = attended[...]
    width = 2432
    total = None
    for n in range(0, width, TILE):
        cols = slice(n, min(n + TILE, width))
        part = jnp.dot(
            rows,
            jnp.concatenate([weight[i, :, cols] for i in range(16)], 0),
            preferred_element_type=f32,
        )
        part = hidden[:, cols].astype(f32) + part + out_bias[cols].astype(f32).reshape(1, -1)
        residual[:, cols] = part
        part = jnp.sum(part, axis=1, keepdims=True)
        total = part if total is None else total + part
    centre = total / width
    total = None
    for n in range(0, width, TILE):
        cols = slice(n, min(n + TILE, width))
        part = residual[:, cols] - centre
        residual[:, cols] = part
        part = jnp.sum(part * part, axis=1, keepdims=True)
        total = part if total is None else total + part
    norm = 1.0 / jnp.sqrt(total / width + 1e-06)
    velocity = None
    for n in range(0, width, TILE):
        cols = slice(n, min(n + TILE, width))
        modulated = residual[:, cols] * norm * (1.0 + scale_ref[:, cols].astype(f32)) + shift_ref[
            :, cols
        ].astype(f32)
        part = lax.dot_general(
            final_weight[:, cols],
            modulated.astype(bf16),
            (((1,), (1,)), ((), ())),
            preferred_element_type=f32,
        )
        velocity = part if velocity is None else velocity + part
    v_stage[0] = velocity[:32].astype(bf16)
    v_stage[1] = velocity[32:].astype(bf16)
    exchange = pltpu.make_async_remote_copy(
        src_ref=v_stage.at[1 - cfg],
        dst_ref=v_recv,
        send_sem=v_sem.at[0],
        recv_sem=v_sem.at[1],
        device_id={"cfg": 1 - cfg},
        device_id_type=MESH,
    )
    exchange.start()
    mine = jnp.where(cfg == 0, velocity[:32], velocity[32:])
    for d in (*along, *across):
        o_copy(d).wait_send()
    for copy in to_core:
        copy.wait_send()
    exchange.wait()
    theirs = v_recv[...].astype(f32)
    cond = jnp.where(cfg == 0, mine, theirs)
    uncond = jnp.where(cfg == 0, theirs, mine)
    guided_ref[...] = uncond + GUIDANCE * (cond - uncond)


def shards(
    q_img,
    k_img,
    v_img,
    text_k,
    text_v,
    text_len,
    head_mask,
    hidden,
    out_weight,
    out_bias,
    final_shift,
    final_scale,
    final_weight,
    latent,
    step_index,
):
    vmem = pltpu.VMEM
    dma = pltpu.SemaphoreType.DMA
    anywhere = pl.BlockSpec(memory_space=pl.ANY)
    whole = pl.BlockSpec(memory_space=pltpu.VMEM)
    guided = pl.pallas_call(
        block_kernel,
        out_shape=jax.ShapeDtypeStruct(latent.shape, f32),
        in_specs=[anywhere] * 13,
        out_specs=whole,
        scratch_shapes=[
            vmem((3, TOKENS, 2560), bf16),
            vmem((2, SLOTS, 384), bf16),
            vmem((8, FEATURES, TOKENS), bf16),
            vmem((8, 2 * FEATURES, TOKENS), bf16),
            vmem((2, 4, FEATURES, TOKENS), bf16),
            vmem((2, 4, FEATURES, TOKENS), bf16),
            vmem((8, FEATURES, TOKENS), bf16),
            vmem((16, 4, 2 * FEATURES, TOKENS), bf16),
            vmem((16, 160, 2432), bf16),
            vmem((24, 128, TILE), bf16),
            vmem((3, SLOTS, 128), bf16),
            vmem((384, SLOTS), bf16),
            vmem((QUERIES, TILE), f32),
            vmem((QUERIES, TILE), f32),
            vmem((QUERIES, TILE), bf16),
            vmem((QUERIES, TILE), bf16),
            vmem((20, 1, TILE), f32),
            vmem((20, 80, TILE), f32),
            vmem((TOKENS, 2432), bf16),
            vmem((TOKENS, 2560), bf16),
            vmem((TOKENS, 2432), f32),
            vmem((2, 32, TOKENS), bf16),
            vmem((32, TOKENS), bf16),
            pltpu.SMEM((1,), jnp.int32),
            pltpu.SMEM((40,), jnp.int32),
            vmem((2432,), bf16),
            vmem((1, 2432), bf16),
            vmem((1, 2432), bf16),
            vmem((64, 2432), bf16),
            dma((14,)),
            dma((8,)),
            dma((8,)),
            dma((8,)),
            dma((8,)),
            dma((12,)),
            dma((16,)),
            dma((8,)),
            dma((8,)),
            dma((8,)),
            dma((8,)),
            dma((14,)),
            dma((14,)),
            dma((2,)),
        ],
        compiler_params=pltpu.CompilerParams(
            collective_id=0, has_side_effects=True, vmem_limit_bytes=60 << 20
        ),
        cost_estimate=pl.CostEstimate(
            flops=40_000_000_000, bytes_accessed=20_000_000, transcendentals=44_000_000
        ),
    )(
        q_img,
        k_img,
        v_img,
        text_k,
        text_v,
        out_weight,
        hidden,
        text_len,
        head_mask,
        out_bias,
        final_shift,
        final_scale,
        final_weight,
    )
    sigma_now = sigma_at(step_index[0])
    sigma_next = sigma_at(step_index[0] + 1)
    denoised = latent - sigma_now * guided
    next_latent = latent + (sigma_next - sigma_now) * guided
    return (next_latent, denoised)


def solution(mesh):
    in_specs = (
        P("cfg", ("seq", "head"), None),
        P("cfg", ("seq", "head"), None),
        P("cfg", ("seq", "head"), None),
        P("cfg", None, None),
        P("cfg", None, None),
        P("cfg"),
        P(),
        P("cfg", ("seq", "head"), None),
        P("head", None),
        P(),
        P("cfg", None),
        P("cfg", None),
        P(),
        P("cfg", ("seq", "head")),
        P(),
    )
    out_specs = (P("cfg", ("seq", "head")), P("cfg", ("seq", "head")))
    return jax.shard_map(shards, mesh=mesh, in_specs=in_specs, out_specs=out_specs, check_vma=False)
```
